32 devices in a mesh: ctx: 8 (over z, core), exp: 4 (over y, x).
Axes of the slice: x: 2, y: 2, z: 4, core: 2. Of those that a mesh axis runs over, the one named last changes fastest.
Arguments:
- scan_input: bfloat16 [1024, 4096], P('ctx', 'exp'), may hold values from -6 to 6
- step_size: bfloat16 [1024, 4096], P('ctx', 'exp'), may hold values from 0.5 to 2
- decay_rate: float32 [16, 4096], P(None, 'exp'), may hold values from 2e-06 to 0.1
- input_proj: float32 [16, 1024], P(None, 'ctx'), may hold values from -1.5 to 1.5
- output_proj: float32 [16, 1024], P(None, 'ctx'), may hold values from -0.4 to 0.4
- skip_gain: float32 [4096], P('exp'), may hold values from 0.5 to 1.5
- block_states: float32 [8, 16, 4096], P('ctx', None, 'exp'), may hold values from -24 to 24
- end_grad: float32 [16, 4096], P(None, 'exp'), may hold values from -6 to 6
- scan_grad: bfloat16 [1024, 4096], P('ctx', 'exp'), may hold values from -6 to 6
- moe_grad: bfloat16 [1024, 4096], P(('ctx', 'exp')), may hold values from -6 to 6
- route: int32 [1024, 2], P(('ctx', 'exp')), may hold values from 0 to 15, all different within a row; in each aligned block of 32 rows (0 to 31, 32 to 63, ...) at most 8 rows name the same one
- gate_prob: float32 [1024, 2], P(('ctx', 'exp')), may hold values from 0.1 to 0.9
- w_down: bfloat16 [16, 7168, 4096], P('exp', 'ctx'), may hold values from -0.0625 to 0.0625
- hidden_saved: bfloat16 [16, 256, 7168], P('exp', None, 'ctx'), may hold values from -6 to 6
Outputs:
- input_grad: bfloat16 [1024, 4096], P('ctx', 'exp')
- step_grad: bfloat16 [1024, 4096], P('ctx', 'exp')
- in_proj_grad: float32 [16, 1024], P(None, 'ctx')
- out_proj_grad: float32 [16, 1024], P(None, 'ctx')
- decay_grad: float32 [16, 4096], P(None, 'exp')
- down_grad: bfloat16 [16, 7168, 4096], P('exp', 'ctx')
- hidden_grad: bfloat16 [16, 256, 7168], P('exp', None, 'ctx')
The draws below stay inside these ranges and needn't reach their ends.
Inputs may be any that keep to these rules, and one draw needn't show every extreme that they name: `route`: the experts of one token differ. Within the 32 tokens of one source (aligned blocks of 32 rows) no expert is named more than 8 times, a bound that some block reaches.
All inputs are finite; a program needn't handle non-finite values.
Results may differ from the reference program's by a relative error of at most 0.0049.
Values may be sent and summed in bfloat16 or wider, within the bound.
No kernel may reach another device: no remote copies, remote signals or barrier semaphores. Data moves between devices by JAX's collectives and lax.ppermute only.
A program may use at most 192 MiB of HBM per device.

```python
import math
import jax
import jax.numpy as jnp
import numpy as np
from jax import lax

D = 4096
INNER = 4096
NSTATE = 16
FF = 7168
EXPERTS = 16
TOPK = 2
TOK_CTX = 128
TOKENS = 1024
TOK_MOE = 32
CAP = 8
SLOTS = 256
N_CTX = 8


def shard_levels(rng, extent, split, smallest, high):
    level = 1.0
    for dim, blocks in split:
        heights = jax.random.uniform(jax.random.fold_in(jax.random.fold_in(rng, 6), dim), (blocks,), jnp.float32, smallest / len(split), high / len(split))
        level = level * jnp.repeat(jnp.exp(heights), extent[dim] // blocks).reshape((-1,) + (1,) * (len(extent) - 1 - dim))
    return level


def shared_out(own_key, own, number, rows, number_of, top, most, slope):
    order = jax.random.permutation(own_key, number_of)
    crowded, usual = load_shares(number_of, rows * top, most, slope, True), load_shares(number_of, rows * top, most, slope, False)
    places = jnp.arange(number_of)

    def named(sizes, offset_by):
        used = int((sizes > 0).sum())
        fixed = max(1, used // 4)
        moved = fixed + (places - fixed + offset_by * (used - fixed)) % max(1, number_of - fixed)
        return jnp.zeros((number_of,), jnp.int32).at[order[jnp.where(places < fixed, places, moved)]].set(jnp.asarray(sizes, jnp.int32))

    sizes = jnp.where(number % 4 == 0, named(crowded, number // 4), named(usual, number - number // 4 - 1))
    mixed = jax.random.permutation(jax.random.fold_in(own, 3), number_of)
    giver, taker = mixed[0:number_of // 2 * 2:2], mixed[1:number_of // 2 * 2:2]
    room = jnp.minimum(sizes[giver] - 1, most - sizes[taker]) // 2
    room = jnp.where((giver == order[0]) | (taker == order[0]) | (sizes[taker] == 0), 0, jnp.maximum(room, 0))
    moved = jax.random.randint(jax.random.fold_in(own, 4), (number_of // 2,), 0, 1 << 20) % (room + 1)
    sizes = sizes.at[giver].add(-moved).at[taker].add(moved)
    members = jnp.searchsorted(jnp.cumsum(sizes), jnp.arange(rows * top), side="right").astype(jnp.int32)
    grid = members.reshape(top, rows).T
    grid = grid[jax.random.permutation(jax.random.fold_in(own, 1), rows)]
    offset_by = jax.random.randint(jax.random.fold_in(own, 2), (rows, 1), 0, top)
    return jnp.take_along_axis(grid, (jnp.arange(top)[None, :] + offset_by) % top, axis=1)


def load_shares(number_of, total, most, slope, full):
    weights = [(1 << 20) // math.isqrt(standing ** slope) + 1 for standing in range(1, number_of + 1)]
    largest = most if full else min(most, max(-(-total // number_of), total * weights[0] // sum(weights)))
    least = 1 if total - largest >= number_of - 1 else 0
    given, rest = [largest] + [least] * (number_of - 1), total - largest - least * (number_of - 1)
    while rest > 0:
        candidates = [i for i in range(1, number_of) if given[i] < largest] or [i for i in range(1, number_of) if given[i] < most]
        mass, left = sum([weights[i] for i in candidates]), rest
        for i in candidates:
            more = min(most - given[i], max(1, left * weights[i] // mass), rest)
            given[i] = given[i] + more
            rest = rest - more
    return np.array(given)


def centred(own_key, dims, scale, bound, shards=(), held_as=jnp.bfloat16):
    entries = scale * jax.random.normal(own_key, dims, jnp.float32)
    if shards:
        entries = entries * shard_levels(own_key, dims, shards, -0.22, 0.18)
    return jnp.clip(entries, -bound, bound).astype(held_as)


def setup_inputs(seed: int = 0) -> dict:
    seeds = jax.random.split(jax.random.key(seed), 15)
    scan_input = centred(seeds[0], (TOKENS, INNER), 1.0, 6.0, ((0, 8), (1, 4)))
    step_size = jnp.clip(jnp.exp(math.log(2.0) - 1.3862944 * jax.random.uniform(seeds[1], (TOKENS, INNER), jnp.float32) ** shard_levels(seeds[1], (TOKENS, INNER), ((0, 8), (1, 4)), -0.2, 0.2)), 0.5, 2.0).astype(jnp.bfloat16)
    decay_rate = jnp.clip(jnp.exp(math.log(0.1) - 10.819778 * jax.random.uniform(seeds[2], (NSTATE, INNER), jnp.float32) ** shard_levels(seeds[2], (NSTATE, INNER), ((1, 4),), -0.2, 0.2)), 1.9999999949504854e-06, 0.1)
    input_proj = centred(seeds[3], (NSTATE, TOKENS), 0.25, 1.5, ((1, 8),), jnp.float32)
    output_proj = centred(seeds[4], (NSTATE, TOKENS), 0.0625, 0.4, ((1, 8),), jnp.float32)
    skip_gain = jnp.clip(0.5 + 1.0 * jax.random.uniform(seeds[5], (INNER,), jnp.float32) ** shard_levels(seeds[5], (INNER,), ((0, 4),), -0.2, 0.2), 0.5, 1.5)
    block_states = centred(seeds[6], (N_CTX, NSTATE, INNER), 4.0, 24.0, ((0, 8), (2, 4)), jnp.float32)
    end_grad = centred(seeds[7], (NSTATE, INNER), 1.0, 6.0, ((1, 4),), jnp.float32)
    scan_grad = centred(seeds[8], (TOKENS, INNER), 1.0, 6.0, ((0, 8), (1, 4)))
    moe_grad = centred(seeds[9], (TOKENS, D), 1.0, 6.0, ((0, 32),))
    route_keys = jax.random.split(jax.random.fold_in(seeds[10], 1), TOKENS // TOK_MOE)
    route_turns = jax.random.permutation(jax.random.fold_in(seeds[10], 3), TOKENS // TOK_MOE)
    route = jax.vmap(lambda own, number: shared_out(jax.random.fold_in(seeds[10], 2), own, number, TOK_MOE, EXPERTS, TOPK, CAP, 2))(route_keys, route_turns).reshape((TOKENS, TOPK))
    gate_prob = jnp.clip(0.1 + 0.79999997 * jax.random.uniform(seeds[11], (TOKENS, TOPK), jnp.float32) ** shard_levels(seeds[11], (TOKENS, TOPK), ((0, 32),), -0.2, 0.2), 0.1, 0.9)
    w_down = centred(seeds[12], (EXPERTS, FF, D), FF ** -0.5, 0.0625, ((0, 4), (1, 8)))
    hidden_saved = centred(seeds[13], (EXPERTS, SLOTS, FF), 1.0, 6.0, ((0, 4), (2, 8)))
    return dict(scan_input=scan_input, step_size=step_size, decay_rate=decay_rate, input_proj=input_proj, output_proj=output_proj, skip_gain=skip_gain, block_states=block_states, end_grad=end_grad, scan_grad=scan_grad, moe_grad=moe_grad, route=route, gate_prob=gate_prob, w_down=w_down, hidden_saved=hidden_saved)


def reference(scan_input, step_size, decay_rate, input_proj, output_proj, skip_gain, block_states, end_grad, scan_grad, moe_grad, route, gate_prob, w_down, hidden_saved):
    inputs_all = scan_input.astype(jnp.float32).reshape(N_CTX, TOK_CTX, INNER)
    steps_all = step_size.astype(jnp.float32).reshape(N_CTX, TOK_CTX, INNER)
    grads_all = scan_grad.astype(jnp.float32).reshape(N_CTX, TOK_CTX, INNER)
    in_mats = input_proj.reshape(NSTATE, N_CTX, TOK_CTX).transpose(1, 2, 0)
    out_mats = output_proj.reshape(NSTATE, N_CTX, TOK_CTX).transpose(1, 2, 0)

    def one_block(incoming, blockdata):
        inputs, steps, bmats, cmats, first_state, grads = blockdata
        decays = jnp.exp(-steps[:, None, :] * decay_rate[None])
        driving = (steps * inputs)[:, None, :] * bmats[:, :, None]

        def forward_step(state, element):
            state = element[0] * state + element[1]
            return state, state

        _, states = lax.scan(forward_step, first_state, (decays, driving))
        before = jnp.concatenate([first_state[None], states[:-1]], axis=0)
        sources = cmats[:, :, None] * grads[:, None, :]

        def backward_step(running, element):
            value = element[1] + running
            return element[0] * value, value

        outgoing, adjoint = lax.scan(backward_step, incoming, (decays, sources), reverse=True)
        input_part = steps * jnp.sum(bmats[:, :, None] * adjoint, axis=1) + skip_gain[None] * grads
        step_part = jnp.sum(adjoint * (bmats[:, :, None] * inputs[:, None, :] - decay_rate[None] * decays * before), axis=1)
        in_part = jnp.sum(adjoint * (steps * inputs)[:, None, :], axis=2)
        out_part = jnp.sum(states * grads[:, None, :], axis=2)
        rate_part = jnp.sum(adjoint * (-steps[:, None, :] * decays * before), axis=0)
        return outgoing, (input_part.astype(jnp.bfloat16), step_part.astype(jnp.bfloat16), in_part, out_part, rate_part)

    _, results = lax.scan(one_block, end_grad, (inputs_all, steps_all, in_mats, out_mats, block_states, grads_all), reverse=True)
    input_grad = results[0].reshape(TOKENS, INNER)
    step_grad = results[1].reshape(TOKENS, INNER)
    in_proj_grad = results[2].transpose(2, 0, 1).reshape(NSTATE, TOKENS)
    out_proj_grad = results[3].transpose(2, 0, 1).reshape(NSTATE, TOKENS)
    decay_grad = jnp.sum(results[4], axis=0)

    sources_count = TOKENS // TOK_MOE
    pairs_source = TOK_MOE * TOPK
    weighted = (gate_prob[:, :, None] * moe_grad.astype(jnp.float32)[:, None, :]).astype(jnp.bfloat16)
    weighted = weighted.reshape(TOKENS * TOPK, D)
    experts_of = route.reshape(sources_count, pairs_source)
    onehot = (experts_of[:, :, None] == jnp.arange(EXPERTS, dtype=jnp.int32)[None, None, :]).astype(jnp.int32)
    earlier = jnp.cumsum(onehot, axis=1) - onehot
    ranks = jnp.sum(earlier * onehot, axis=2)
    source_ids = jnp.arange(sources_count, dtype=jnp.int32)[:, None]
    slot_ids = (source_ids * CAP + ranks).reshape(-1).astype(jnp.int32)
    expert_ids = experts_of.reshape(-1).astype(jnp.int32)
    dispatched = jnp.zeros((EXPERTS, SLOTS, D), jnp.bfloat16).at[expert_ids, slot_ids].set(weighted)

    def per_expert(element):
        buffer, weight, saved = element
        weight_part = jnp.dot(saved.T, buffer, preferred_element_type=jnp.float32).astype(jnp.bfloat16)
        saved_part = jnp.dot(buffer, weight.T, preferred_element_type=jnp.float32).astype(jnp.bfloat16)
        return weight_part, saved_part

    down_grad, hidden_grad = lax.map(per_expert, (dispatched, w_down, hidden_saved))
    return (input_grad, step_grad, in_proj_grad, out_proj_grad, decay_grad, down_grad, hidden_grad)
```

```python
import functools
import math

import jax
import jax.numpy as jnp
from jax import lax
from jax.experimental import pallas as pl
from jax.experimental.pallas import tpu as pltpu
from jax.sharding import PartitionSpec as P

EXPERTS = 16
F32 = jnp.float32
BF16 = jnp.bfloat16
LOG2E = math.log2(math.e)
LN2 = math.log(2.0)
LANES = 128
EXTRA = 128
CHUNK = 16
PARTS = 2
VMEM_BYTES = 56 * 1024 * 1024
BOTH = ("ctx", "exp")


def lane_column(matrix, index):
    places = jnp.full(matrix.shape, index, jnp.int32)
    return jnp.take_along_axis(matrix, places, axis=1, mode="promise_in_bounds")


def widen(column, width):
    return jnp.concatenate([column] * (width // LANES), axis=1)


def fold_lanes(value):
    total = value[:, :LANES]
    for start in range(LANES, value.shape[1], LANES):
        total = total + value[:, start : start + LANES]
    return total


def lane_sums(partials):
    return lax.dot_general(
        jnp.ones((8, LANES), F32),
        partials,
        (((1,), (1,)), ((), ())),
        precision=lax.Precision.HIGHEST,
        preferred_element_type=F32,
    )


def seed_kernel(step_ref, grad_ref, rate_ref, cmat_ref, out_ref, step_s, grad_s):
    tokens, width = step_ref.shape
    states = rate_ref.shape[0]
    step_s[...] = step_ref[...].astype(F32)
    grad_s[...] = grad_ref[...].astype(F32)
    scaled = rate_ref[...] * -LOG2E
    cmat = cmat_ref[...]
    unroll = 8

    def several(i, running):
        for k in range(unroll):
            t = tokens - 1 - (i * unroll + k)
            ccol = widen(lane_column(cmat, t), width)
            stp = step_s[pl.ds(t, 1), :]
            grad = grad_s[pl.ds(t, 1), :]
            running = jnp.exp2(scaled * stp) * (ccol * grad + running)
        return running

    running = lax.fori_loop(0, tokens // unroll, several, jnp.zeros((states, width), F32))
    out_ref[0:states, :] = running
    out_ref[states : states + 1, :] = jnp.sum(step_s[...], axis=0, keepdims=True)


def forward_kernel(
    step_ref, inp_ref, grad_ref, rate_ref, bmat_ref, first_ref, before_ref, cols_ref,
    step_s, drive_s, grad_s, total_s,
):
    tokens, width = step_ref.shape
    states = rate_ref.shape[0]
    steps = step_ref[...].astype(F32)
    step_s[...] = steps
    drive_s[...] = steps * inp_ref[...].astype(F32)
    grad_s[...] = grad_ref[...].astype(F32)
    scaled = rate_ref[...] * -LOG2E
    bmat = bmat_ref[...]
    unroll = 8

    @pl.when(pl.program_id(0) == 0)
    def _():
        total_s[...] = jnp.zeros_like(total_s)

    def several(i, state):
        for k in range(unroll):
            t = i * unroll + k
            rows = pl.ds(pl.multiple_of(t * states, states), states)
            before_ref[rows, :] = state.astype(BF16)
            bcol = widen(lane_column(bmat, t), width)
            state = jnp.exp2(scaled * step_s[pl.ds(t, 1), :]) * state + bcol * drive_s[pl.ds(t, 1), :]
            total_s[rows, :] += fold_lanes(state * grad_s[pl.ds(t, 1), :])
        return state

    lax.fori_loop(0, tokens // unroll, several, first_ref[0])

    @pl.when(pl.program_id(0) == pl.num_programs(0) - 1)
    def _():
        cols_ref[...] = lane_sums(total_s[...])


def adjoint_kernel(
    step_ref, inp_ref, grad_ref, rate_ref, bdiag_ref, cmat_ref, skip_ref, enter_ref, before_ref,
    input_ref, stepg_ref, cols_ref, rateg_ref,
    step_s, drive_s, grad_s, total_s, adj_s, rated_s,
):
    tokens, width = step_ref.shape
    states = rate_ref.shape[0]
    steps = step_ref[...].astype(F32)
    step_s[...] = steps
    drive_s[...] = steps * inp_ref[...].astype(F32)
    grad_s[...] = grad_ref[...].astype(F32)
    scaled = rate_ref[...] * -LOG2E
    cmat = cmat_ref[...]
    skip = skip_ref[...]
    chunks = tokens // CHUNK
    rows_of = lax.broadcasted_iota(jnp.int32, (CHUNK, CHUNK * states), 0)
    cols_of = lax.broadcasted_iota(jnp.int32, (CHUNK, CHUNK * states), 1)
    ones_diag = jnp.where(lax.div(cols_of, states) == rows_of, 1.0, 0.0).astype(BF16)

    @pl.when(pl.program_id(0) == 0)
    def _():
        total_s[...] = jnp.zeros_like(total_s)

    def chunk(i, carry):
        running, rate_acc = carry
        base = (chunks - 1 - i) * CHUNK
        for k in reversed(range(CHUNK)):
            t = base + k
            rows = pl.ds(pl.multiple_of(t * states, states), states)
            held = slice(k * states, (k + 1) * states)
            stp = step_s[pl.ds(t, 1), :]
            ccol = widen(lane_column(cmat, t), width)
            adjoint = ccol * grad_s[pl.ds(t, 1), :] + running
            adj_s[held, :] = adjoint.astype(BF16)
            total_s[rows, :] += fold_lanes(adjoint * drive_s[pl.ds(t, 1), :])
            running = jnp.exp2(scaled * stp) * adjoint
            weighted = running * before_ref[rows, :].astype(F32)
            rated_s[held, :] = (scaled * weighted).astype(BF16)
            rate_acc = rate_acc + stp * weighted
        rows = pl.ds(pl.multiple_of(base, CHUNK), CHUNK)
        driven = jnp.dot(bdiag_ref[rows, :], adj_s[...], preferred_element_type=F32)
        rated = jnp.dot(ones_diag, rated_s[...], preferred_element_type=F32)
        input_ref[rows, :] = (step_s[rows, :] * driven + skip * grad_s[rows, :]).astype(BF16)
        stepg_ref[rows, :] = (inp_ref[rows, :].astype(F32) * driven + LN2 * rated).astype(BF16)
        return running, rate_acc

    enter = enter_ref[...]
    _, rate_acc = lax.fori_loop(0, chunks, chunk, (enter, jnp.zeros_like(enter)))
    rateg_ref[...] = -rate_acc

    @pl.when(pl.program_id(0) == pl.num_programs(0) - 1)
    def _():
        cols_ref[...] = lane_sums(total_s[...])


def scan_call(kernel, name, width, tokens, states, ins, outs, scratch, flops):
    block = min(512, width)
    kinds = {
        "tok": pl.BlockSpec((tokens, block), lambda j: (0, j)),
        "rate": pl.BlockSpec((states, block), lambda j: (0, j)),
        "seed": pl.BlockSpec((states + 1, block), lambda j: (0, j)),
        "mat": pl.BlockSpec((states, tokens), lambda j: (0, 0)),
        "diag": pl.BlockSpec((tokens, CHUNK * states), lambda j: (0, 0)),
        "first": pl.BlockSpec((1, states, block), lambda j: (0, 0, j)),
        "skip": pl.BlockSpec((1, block), lambda j: (0, j)),
        "state": pl.BlockSpec((tokens * states, block), lambda j: (0, j)),
        "cols": pl.BlockSpec((8, tokens * states), lambda j: (0, 0)),
    }
    shapes = {
        "tok": jax.ShapeDtypeStruct((tokens, width), BF16),
        "rate": jax.ShapeDtypeStruct((states, width), F32),
        "seed": jax.ShapeDtypeStruct((states + 1, width), F32),
        "state": jax.ShapeDtypeStruct((tokens * states, width), BF16),
        "cols": jax.ShapeDtypeStruct((8, tokens * states), F32),
    }
    scratches = {
        "row": pltpu.VMEM((tokens, block), F32),
        "total": pltpu.VMEM((tokens * states, LANES), F32),
        "chunk": pltpu.VMEM((CHUNK * states, block), BF16),
    }
    return pl.pallas_call(
        kernel,
        name=name,
        grid=(width // block,),
        in_specs=[kinds[kind] for kind in ins],
        out_specs=[kinds[kind] for kind in outs],
        out_shape=[shapes[kind] for kind in outs],
        scratch_shapes=[scratches[kind] for kind in scratch],
        compiler_params=pltpu.CompilerParams(vmem_limit_bytes=32 * 1024 * 1024),
        cost_estimate=pl.CostEstimate(
            flops=flops, bytes_accessed=6 * tokens * width, transcendentals=tokens * states * width
        ),
    )


def entering_adjoint(seeded, decay_rate, end_grad):
    states = decay_rate.shape[0]
    count = lax.axis_size("ctx")
    position = lax.axis_index("ctx")
    total = seeded
    later = jnp.zeros_like(seeded)

    def after(first, second):
        steps = first[states:] + second[states:]
        seed = jnp.exp(-decay_rate * first[states:]) * second[:states] + first[:states]
        return jnp.concatenate([seed, steps], axis=0)

    bit = 1
    while bit < count:
        other = lax.ppermute(total, "ctx", [(i, i ^ bit) for i in range(count)])
        low = (position & bit) == 0
        later = jnp.where(low, after(later, other), later)
        if 2 * bit < count:
            total = after(jnp.where(low, total, other), jnp.where(low, other, total))
        bit *= 2
    return jnp.exp(-decay_rate * later[states:]) * end_grad + later[:states]


def pack_kernel(widths, local, capacity, place_ref, grad_ref, route_ref, gate_ref, *out_refs):
    tokens = route_ref.shape[0]
    route = route_ref[...]
    gate = gate_ref[...]
    experts_of = lax.broadcasted_iota(jnp.int32, (tokens, EXPERTS), 1)
    first, second = (experts_of == route[:, 0:1]), (experts_of == route[:, 1:2])
    named = (first | second).astype(F32)
    row = lax.broadcasted_iota(jnp.int32, (tokens, tokens), 0)
    col = lax.broadcasted_iota(jnp.int32, (tokens, tokens), 1)
    earlier = jnp.dot(
        jnp.where(col < row, 1.0, 0.0).astype(BF16), named.astype(BF16), preferred_element_type=F32
    )
    lane = lax.broadcasted_iota(jnp.int32, (tokens, EXTRA), 1)
    extra = jnp.zeros((tokens, EXTRA), F32)
    sources = place_ref[1]
    for j, chosen in enumerate((first, second)):
        rank = jnp.sum(jnp.where(chosen, earlier, 0.0), axis=1, keepdims=True)
        expert = route[:, j : j + 1]
        owner = lax.div(expert, local)
        slot = ((expert - owner * local) * sources + place_ref[0]) * capacity
        prob = gate[:, j : j + 1]
        high = prob.astype(BF16).astype(F32)
        middle = (prob - high).astype(BF16).astype(F32)
        low = prob - high - middle
        fields = (owner.astype(F32), slot.astype(F32) + rank, high, middle, low)
        for k, field in enumerate(fields):
            extra = jnp.where(lane == 8 * j + k, field, extra)
    start = 0
    for width, out_ref in zip(widths, out_refs):
        out_ref[:, :width] = grad_ref[:, start : start + width]
        start += width
    out_refs[0][:, widths[0] :] = extra.astype(BF16)


def pack_tokens(moe_grad, route, gate_prob, widths, local, capacity):
    tokens = moe_grad.shape[0]
    around = lax.axis_size("exp")
    place = jnp.stack(
        [(lax.axis_index("ctx") % 2) * around + lax.axis_index("exp"), 2 * around]
    ).astype(jnp.int32)
    vmem = pl.BlockSpec(memory_space=pltpu.VMEM)
    outs = [
        jax.ShapeDtypeStruct((tokens, width + (EXTRA if p == 0 else 0)), BF16)
        for p, width in enumerate(widths)
    ]
    return pl.pallas_call(
        functools.partial(pack_kernel, widths, local, capacity),
        name="pack_tokens",
        in_specs=[pl.BlockSpec(memory_space=pltpu.SMEM), vmem, vmem, vmem],
        out_specs=[vmem] * len(outs),
        out_shape=outs,
    )(place, moe_grad, route, gate_prob)


def token_hops():
    def pairing(partner):
        pairs = []
        for i in range(32):
            z, c, y, x = i // 8, (i // 4) % 2, (i // 2) % 2, i % 2
            z, c, y, x = partner(z, c, y, x)
            pairs.append((i, ((z * 2 + c) * 2 + y) * 2 + x))
        return pairs

    return (
        pairing(lambda z, c, y, x: (z ^ 2, c, y, x)),
        pairing(lambda z, c, y, x: (z ^ 1, c, y, x)),
        pairing(lambda z, c, y, x: (z, c, y, x ^ 1) if c == 0 else (z, c, y ^ 1, x)),
        pairing(lambda z, c, y, x: (z, c, y ^ 1, x) if c == 0 else (z, c, y, x ^ 1)),
        pairing(lambda z, c, y, x: (z, c ^ 1, y, x)),
    )


def spread_tokens(packed):
    tokens, width = packed.shape
    far_z, near_z, plane_one, plane_two, core = token_hops()
    held = packed[None, None]
    held = jnp.concatenate([held, lax.ppermute(held, BOTH, far_z)], axis=0)
    held = jnp.concatenate([held, lax.ppermute(held, BOTH, near_z)], axis=0)
    held = jnp.concatenate([held, lax.ppermute(held, BOTH, plane_one)], axis=1)
    held = held.reshape(4 * 2 * tokens, width)
    other = lax.ppermute(held, BOTH, plane_two)
    pieces = [held, other, lax.ppermute(held, BOTH, core), lax.ppermute(other, BOTH, core)]
    return pieces


def expert_kernel(first, last, zs, place_ref, *refs):
    pieces, refs = refs[:4], refs[4:]
    extras, refs = refs[:4], refs[4:]
    saved_ref, w_ref, refs = refs[0], refs[1], refs[2:]
    if not first:
        sum_ref, refs = refs[0], refs[2:]
    down_ref, hidden_ref, pick_s, gate_s, slots_s, acc_s = refs
    d, l = pl.program_id(0), pl.program_id(1)
    local, slots, block = slots_s.shape
    per_z = slots // zs
    rows_z = pieces[0].shape[0] // zs

    @pl.when((d == 0) & (l == 0))
    def _():
        for jz in range(zs):
            held = jnp.concatenate([ref[jz * rows_z : (jz + 1) * rows_z, :] for ref in extras], axis=0)
            table = held.astype(F32).T
            row = lax.broadcasted_iota(jnp.int32, (local * per_z, held.shape[0]), 0).astype(F32)
            me = place_ref[1].astype(F32)
            pick = jnp.zeros(row.shape, F32)
            gate = jnp.zeros(row.shape, F32)
            for j in range(2):
                owner, slot, high, middle, low = [table[8 * j + k : 8 * j + k + 1, :] for k in range(5)]
                hit = (jnp.where(owner == me, slot, -1.0)) == row
                pick = jnp.where(hit, 1.0, pick)
                gate = jnp.where(hit, (high + middle) + low, gate)
            pick_s[jz] = pick.astype(BF16)
            gate_s[jz] = jnp.broadcast_to(jnp.sum(gate, axis=1, keepdims=True), (local * per_z, LANES))

    @pl.when(l == 0)
    def _():
        for jz in range(zs):
            held = jnp.concatenate([ref[jz * rows_z : (jz + 1) * rows_z, :] for ref in pieces], axis=0)
            chosen = jnp.dot(pick_s[jz], held, preferred_element_type=F32)
            value = (chosen * widen(gate_s[jz], block)).astype(BF16)
            z = place_ref[0] ^ (2 * (jz % 2) + jz // 2)
            rows = pl.ds(pl.multiple_of(z * per_z, per_z), per_z)
            for expert in range(local):
                slots_s[expert, rows, :] = value[expert * per_z : (expert + 1) * per_z, :]

    mine = slots_s[l]
    down_ref[0] = jnp.dot(saved_ref[l], mine, preferred_element_type=F32).astype(BF16)
    part = lax.dot_general(mine, w_ref[0], (((1,), (1,)), ((), ())), preferred_element_type=F32)

    @pl.when(d == 0)
    def _():
        acc_s[l] = part if first else sum_ref[l] + part

    @pl.when(d > 0)
    def _():
        acc_s[l] += part

    @pl.when(d == pl.num_programs(0) - 1)
    def _():
        hidden_ref[l] = acc_s[l].astype(hidden_ref.dtype)


def expert_call(part, parts, width, place, pieces, extras, saved_t, w_down, carried):
    local, hidden, full = w_down.shape
    slots = saved_t.shape[2]
    zs = 4
    block = 1024
    rows = pieces[0].shape[0]
    first, last = part == 0, part == parts - 1
    at = part * width // block
    extra_at = width // EXTRA
    whole = lambda d, l: (0, 0, 0)
    in_specs = [pl.BlockSpec(memory_space=pltpu.SMEM)]
    in_specs += [pl.BlockSpec((rows, block), lambda d, l: (0, d))] * 4
    in_specs += [pl.BlockSpec((rows, EXTRA), lambda d, l: (0, extra_at))] * 4
    in_specs += [pl.BlockSpec((local, hidden, slots), whole)]
    in_specs += [pl.BlockSpec((1, hidden, block), lambda d, l: (l, 0, at + d))]
    operands = [place, *pieces, *extras, saved_t, w_down]
    aliases = {}
    if not first:
        in_specs += [pl.BlockSpec((local, slots, hidden), whole), pl.BlockSpec(memory_space=pl.ANY)]
        operands += [carried[1], carried[0]]
        aliases = {len(operands) - 1: 0}
    flops = 4 * local * hidden * slots * width
    return pl.pallas_call(
        functools.partial(expert_kernel, first, last, zs),
        name=f"experts_{part}",
        grid=(width // block, local),
        in_specs=in_specs,
        out_specs=[
            pl.BlockSpec((1, hidden, block), lambda d, l: (l, 0, at + d)),
            pl.BlockSpec((local, slots, hidden), whole),
        ],
        out_shape=[
            jax.ShapeDtypeStruct((local, hidden, full), BF16),
            jax.ShapeDtypeStruct((local, slots, hidden), BF16 if last else F32),
        ],
        scratch_shapes=[
            pltpu.VMEM((zs, 4 * rows // zs, 4 * rows // zs), BF16),
            pltpu.VMEM((zs, 4 * rows // zs, LANES), F32),
            pltpu.VMEM((local, slots, block), BF16),
            pltpu.VMEM((local, slots, hidden), F32),
        ],
        input_output_aliases=aliases,
        compiler_params=pltpu.CompilerParams(vmem_limit_bytes=VMEM_BYTES),
        cost_estimate=pl.CostEstimate(
            flops=flops, bytes_accessed=4 * local * hidden * width, transcendentals=0
        ),
    )(*operands)


def slot_buffer(moe_grad, route, gate_prob, capacity):
    pair_count = route.shape[0] * route.shape[1]
    weighted = (gate_prob[:, :, None] * moe_grad.astype(F32)[:, None, :]).astype(BF16)
    weighted = weighted.reshape(pair_count, moe_grad.shape[1])
    flat_route = route.reshape(pair_count)
    onehot = (flat_route[:, None] == jnp.arange(EXPERTS, dtype=jnp.int32)[None, :]).astype(jnp.int32)
    ranks = jnp.sum((jnp.cumsum(onehot, axis=0) - onehot) * onehot, axis=1)
    target = flat_route * capacity + ranks
    placing = (target[:, None] == jnp.arange(EXPERTS * capacity, dtype=jnp.int32)[None, :]).astype(BF16)
    buffer = jnp.einsum("ps,pd->sd", placing, weighted, preferred_element_type=F32).astype(BF16)
    return buffer.reshape(EXPERTS, capacity, moe_grad.shape[1])


def experts_by_slots(moe_grad, route, gate_prob, w_down, hidden_saved, capacity):
    buffer = slot_buffer(moe_grad, route, gate_prob, capacity)
    rows = lax.all_to_all(buffer, "exp", split_axis=0, concat_axis=1, tiled=True)
    rows = lax.all_gather(rows, "ctx", axis=1, tiled=True)
    down = jnp.einsum("lrf,lrd->lfd", hidden_saved, rows, preferred_element_type=F32).astype(BF16)
    hidden = jnp.einsum("lrd,lfd->lrf", rows, w_down, preferred_element_type=F32).astype(BF16)
    return down, hidden


def experts_by_tokens(moe_grad, route, gate_prob, w_down, hidden_saved, capacity):
    local = w_down.shape[0]
    width = moe_grad.shape[1] // PARTS
    packed = pack_tokens(moe_grad, route, gate_prob, (width,) * PARTS, local, capacity)
    place = jnp.stack([lax.axis_index("ctx") // 2, lax.axis_index("exp")]).astype(jnp.int32)
    saved_t = jnp.swapaxes(hidden_saved, 1, 2)
    spread = [spread_tokens(part) for part in packed]
    carried = None
    for part, pieces in enumerate(spread):
        carried = expert_call(part, PARTS, width, place, pieces, spread[0], saved_t, w_down, carried)
    return carried


def body(
    scan_input, step_size, decay_rate, input_proj, output_proj, skip_gain, block_states, end_grad,
    scan_grad, moe_grad, route, gate_prob, w_down, hidden_saved,
):
    tokens, width = scan_input.shape
    states = decay_rate.shape[0]
    call = functools.partial(scan_call, width=width, tokens=tokens, states=states)
    (seeded,) = call(
        seed_kernel, "seed_scan", ins=("tok", "tok", "rate", "mat"), outs=("seed",),
        scratch=("row", "row"), flops=5 * tokens * states * width,
    )(step_size, scan_grad, decay_rate, output_proj)
    before, out_cols = call(
        forward_kernel, "forward_scan", ins=("tok", "tok", "tok", "rate", "mat", "first"),
        outs=("state", "cols"), scratch=("row", "row", "row", "total"),
        flops=7 * tokens * states * width,
    )(step_size, scan_input, scan_grad, decay_rate, input_proj, block_states)
    entering = entering_adjoint(seeded, decay_rate, end_grad)
    spots = jnp.arange(CHUNK * states, dtype=jnp.int32)[None, :] // states
    own = jnp.arange(tokens, dtype=jnp.int32)[:, None] % CHUNK
    bdiag = jnp.where(spots == own, jnp.tile(input_proj.T, (1, CHUNK)), 0.0).astype(BF16)
    input_grad, step_grad, in_cols, rate_local = call(
        adjoint_kernel, "adjoint_scan",
        ins=("tok", "tok", "tok", "rate", "diag", "mat", "skip", "rate", "state"),
        outs=("tok", "tok", "cols", "rate"),
        scratch=("row", "row", "row", "total", "chunk", "chunk"),
        flops=12 * tokens * states * width,
    )(
        step_size, scan_input, scan_grad, decay_rate, bdiag, output_proj, skip_gain[None],
        entering, before,
    )
    both = jnp.stack([in_cols[0], out_cols[0]])
    both = lax.psum(both, "exp").reshape(2, tokens, states).swapaxes(1, 2)
    decay_grad = lax.psum(rate_local, "ctx")
    sources = lax.axis_size("ctx") * lax.axis_size("exp")
    capacity = hidden_saved.shape[1] // sources
    if lax.axis_size("ctx") == 8 and lax.axis_size("exp") == 4:
        experts = experts_by_tokens
    else:
        experts = experts_by_slots
    down_grad, hidden_grad = experts(moe_grad, route, gate_prob, w_down, hidden_saved, capacity)
    return (input_grad, step_grad, both[0], both[1], decay_grad, down_grad, hidden_grad)


def solution(mesh):
    placed = (
        P("ctx", "exp"),
        P("ctx", "exp"),
        P(None, "exp"),
        P(None, "ctx"),
        P(None, "ctx"),
        P("exp"),
        P("ctx", None, "exp"),
        P(None, "exp"),
        P("ctx", "exp"),
        P(("ctx", "exp"), None),
        P(("ctx", "exp"), None),
        P(("ctx", "exp"), None),
        P("exp", "ctx", None),
        P("exp", None, "ctx"),
    )
    return jax.shard_map(
        body,
        mesh=mesh,
        in_specs=placed,
        out_specs=(
            P("ctx", "exp"),
            P("ctx", "exp"),
            P(None, "ctx"),
            P(None, "ctx"),
            P(None, "exp"),
            P("exp", "ctx", None),
            P("exp", None, "ctx"),
        ),
        check_vma=False,
    )
```

```python
import functools
import math

import jax
import jax.numpy as jnp
from jax import lax
from jax.experimental import pallas as pl
from jax.experimental.pallas import tpu as pltpu
from jax.sharding import PartitionSpec as P

EXPERTS = 16
F32 = jnp.float32
BF16 = jnp.bfloat16
LOG2E = math.log2(math.e)
LN2 = math.log(2.0)
LANES = 128
EXTRA = 128
CHUNK = 16
COLUMNS = 512
PIECE = 1024
WIDTHS = (2048, 2048)
SMALL_VMEM = 4 * 1024 * 1024
BOTH = ("ctx", "exp")


def lane_column(matrix, index):
    places = jnp.full(matrix.shape, index, jnp.int32)
    return jnp.take_along_axis(matrix, places, axis=1, mode="promise_in_bounds")


def widen(column, width):
    return jnp.concatenate([column] * (width // LANES), axis=1)


def fold_lanes(value):
    total = value[:, :LANES]
    for start in range(LANES, value.shape[1], LANES):
        total = total + value[:, start : start + LANES]
    return total


def lane_sums(base, partials_s, sums):
    states = sums.shape[0]
    partials = partials_s[...]
    ones = jnp.ones((LANES, sums.shape[1]), BF16)
    high = partials.astype(BF16)
    low = (partials - high.astype(F32)).astype(BF16)
    total = jnp.dot(high, ones, preferred_element_type=F32)
    total += jnp.dot(low, ones, preferred_element_type=F32)
    lane = lax.broadcasted_iota(jnp.int32, sums.shape, 1)
    for k in range(CHUNK):
        sums = jnp.where(lane == base + k, total[k * states : (k + 1) * states, :], sums)
    return sums


def seed_kernel(
    step_ref, inp_ref, grad_ref, rate_ref, cmat_ref, out_ref, step_v, drive_v, inp_v, grad_v
):
    tokens, width = step_ref.shape
    states = rate_ref.shape[0]
    block = pl.ds(pl.multiple_of(pl.program_id(0) * width, width), width)
    steps = step_ref[...].astype(F32)
    inputs = inp_ref[...].astype(F32)
    step_v[:, block] = steps
    drive_v[:, block] = steps * inputs
    inp_v[:, block] = inputs
    grad_v[:, block] = grad_ref[...].astype(F32)
    scaled = rate_ref[...] * -LOG2E
    cmat = cmat_ref[...]
    unroll = CHUNK

    def several(i, running):
        for k in range(unroll):
            t = tokens - 1 - (i * unroll + k)
            ccol = widen(lane_column(cmat, t), width)
            stp = step_v[pl.ds(t, 1), block]
            grad = grad_v[pl.ds(t, 1), block]
            running = jnp.exp2(scaled * stp) * (ccol * grad + running)
        return running

    running = lax.fori_loop(0, tokens // unroll, several, jnp.zeros((states, width), F32))
    out_ref[0:states, :] = running
    out_ref[states : states + 1, :] = jnp.sum(steps, axis=0, keepdims=True)


def fetch_copies(fetch, refs):
    if fetch is None:
        return [], refs
    at, width, outs = fetch
    w_ref, held_v, sems = refs[0], refs[1 + outs], refs[-1]
    refs = [*refs[1 : 1 + outs], *refs[2 + outs : -1]]
    copies = [
        pltpu.make_async_copy(w_ref.at[l, :, pl.ds(at, width)], held_v.at[l], sems.at[l])
        for l in range(held_v.shape[0])
    ]
    return copies, refs


def forward_kernel(
    fetch, step_v, drive_v, grad_v, rate_ref, bmat_ref, first_ref, *refs
):
    copies, refs = fetch_copies(fetch, refs)
    before_v, cols_ref, partials_s = refs
    tokens = step_v.shape[0]
    states, width = rate_ref.shape
    block = pl.ds(pl.multiple_of(pl.program_id(0) * width, width), width)

    @pl.when(pl.program_id(0) == 0)
    def _():
        for copy in copies:
            copy.start()
        cols_ref[...] = jnp.zeros_like(cols_ref)

    scaled = rate_ref[...] * -LOG2E
    bmat = bmat_ref[...]

    def chunk(i, carry):
        state, cols = carry
        base = i * CHUNK
        for k in range(CHUNK):
            t = base + k
            before_v[pl.ds(pl.multiple_of(t * states, states), states), block] = state.astype(BF16)
            bcol = widen(lane_column(bmat, t), width)
            state = (
                jnp.exp2(scaled * step_v[pl.ds(t, 1), block]) * state
                + bcol * drive_v[pl.ds(t, 1), block]
            )
            partials_s[k * states : (k + 1) * states, :] = fold_lanes(
                state * grad_v[pl.ds(t, 1), block]
            )
        return state, lane_sums(base, partials_s, cols)

    _, cols = lax.fori_loop(
        0, tokens // CHUNK, chunk, (first_ref[0], jnp.zeros(cols_ref.shape, F32))
    )
    cols_ref[...] += cols

    @pl.when(pl.program_id(0) == pl.num_programs(0) - 1)
    def _():
        for copy in copies:
            copy.wait()


def adjoint_kernel(
    fetch, step_v, drive_v, inp_v, grad_v, before_v, rate_ref, bmat_ref, cmat_ref, skip_ref,
    end_ref, later_ref, other_ref, out_cols_ref, *refs
):
    copies, refs = fetch_copies(fetch, refs)
    input_ref, stepg_ref, cols_ref, rateg_ref, adj_s, rated_s, partials_s, bdiag_s = refs
    tokens = step_v.shape[0]
    states, width = rate_ref.shape
    block = pl.ds(pl.multiple_of(pl.program_id(0) * width, width), width)
    rate = rate_ref[...]
    scaled = rate * -LOG2E
    cmat = cmat_ref[...]
    skip = skip_ref[...]
    chunks = tokens // CHUNK
    span = CHUNK * states
    ones_diag = jnp.where(
        lax.div(lax.broadcasted_iota(jnp.int32, (CHUNK, span), 1), states)
        == lax.broadcasted_iota(jnp.int32, (CHUNK, span), 0),
        1.0,
        0.0,
    ).astype(BF16)

    @pl.when(pl.program_id(0) == 0)
    def _():
        for copy in copies:
            copy.start()
        cols_ref[0] = jnp.zeros(cols_ref.shape[1:], F32)
        cols_ref[1] = out_cols_ref[...]
        spread_to = jnp.where(
            lax.rem(lax.broadcasted_iota(jnp.int32, (states, span), 1), states)
            == lax.broadcasted_iota(jnp.int32, (states, span), 0),
            1.0,
            0.0,
        ).astype(BF16)
        own = lax.div(lax.broadcasted_iota(jnp.int32, (tokens, span), 1), states) == lax.rem(
            lax.broadcasted_iota(jnp.int32, (tokens, span), 0), CHUNK
        )
        by_token = bmat_ref[...].T
        high = by_token.astype(BF16)
        low = (by_token - high.astype(F32)).astype(BF16)
        for part, value in enumerate((high, low)):
            spread = jnp.dot(value, spread_to, preferred_element_type=F32)
            bdiag_s[part] = jnp.where(own, spread, 0.0).astype(BF16)

    def chunk(i, carry):
        running, rate_acc, cols = carry
        base = (chunks - 1 - i) * CHUNK
        for k in reversed(range(CHUNK)):
            t = base + k
            held = slice(k * states, (k + 1) * states)
            stp = step_v[pl.ds(t, 1), block]
            ccol = widen(lane_column(cmat, t), width)
            adjoint = ccol * grad_v[pl.ds(t, 1), block] + running
            adj_s[held, :] = adjoint.astype(BF16)
            partials_s[held, :] = fold_lanes(adjoint * drive_v[pl.ds(t, 1), block])
            running = jnp.exp2(scaled * stp) * adjoint
            prior = before_v[pl.ds(pl.multiple_of(t * states, states), states), block]
            weighted = running * prior.astype(F32)
            rated_s[held, :] = (scaled * weighted).astype(BF16)
            rate_acc = rate_acc + stp * weighted
        rows = pl.ds(pl.multiple_of(base, CHUNK), CHUNK)
        adjoints = adj_s[...]
        driven = jnp.dot(bdiag_s[0, rows, :], adjoints, preferred_element_type=F32)
        driven += jnp.dot(bdiag_s[1, rows, :], adjoints, preferred_element_type=F32)
        rated = jnp.dot(ones_diag, rated_s[...], preferred_element_type=F32)
        input_ref[rows, :] = (step_v[rows, block] * driven + skip * grad_v[rows, block]).astype(BF16)
        stepg_ref[rows, :] = (inp_v[rows, block] * driven + LN2 * rated).astype(BF16)
        return running, rate_acc, lane_sums(base, partials_s, cols)

    later = later_ref[...]
    beyond = end_ref[...]

    def through(held, value):
        return jnp.exp(-rate * held[states:]) * value + held[:states]

    passed = through(other_ref[...], beyond)
    beyond = jnp.where(ctx_bit(lax.axis_size("ctx") // 2), passed, beyond)
    enter = through(later, beyond)
    _, rate_acc, cols = lax.fori_loop(
        0, chunks, chunk, (enter, jnp.zeros_like(enter), jnp.zeros(cols_ref.shape[1:], F32))
    )
    rateg_ref[...] = -rate_acc
    cols_ref[0] += cols

    @pl.when(pl.program_id(0) == pl.num_programs(0) - 1)
    def _():
        for copy in copies:
            copy.wait()


def ctx_bit(bit):
    return lax.rem(lax.div(lax.axis_index("ctx"), bit), 2) == 0


def fold_kernel(bit, total_ref, later_ref, other_ref, rate_ref, total_out, later_out):
    states = rate_ref.shape[0]
    low = ctx_bit(bit)
    rate = rate_ref[...]
    total, later, other = total_ref[...], later_ref[...], other_ref[...]

    def after(first, second):
        seed = jnp.exp(-rate * first[states:]) * second[:states] + first[:states]
        return seed, first[states:] + second[states:]

    seed, steps = after(jnp.where(low, total, other), jnp.where(low, other, total))
    total_out[:states, :] = seed
    total_out[states:, :] = steps
    seed, steps = after(later, other)
    later_out[:states, :] = jnp.where(low, seed, later[:states])
    later_out[states:, :] = jnp.where(low, steps, later[states:])


def first_fold_kernel(bit, total_ref, other_ref, rate_ref, total_out, later_out):
    states = rate_ref.shape[0]
    low = ctx_bit(bit)
    rate = rate_ref[...]
    total, other = total_ref[...], other_ref[...]
    first, second = jnp.where(low, total, other), jnp.where(low, other, total)
    total_out[:states, :] = jnp.exp(-rate * first[states:]) * second[:states] + first[:states]
    total_out[states:, :] = first[states:] + second[states:]
    later_out[...] = jnp.where(low, other, 0.0)


def exchanged_seeds(seeded, decay_rate):
    count = lax.axis_size("ctx")
    total, later, totals = seeded, None, []
    bit = 1
    while bit < count:
        other = lax.ppermute(total, "ctx", [(i, i ^ bit) for i in range(count)])
        if 2 * bit == count:
            return later, other, totals
        held = [total, other] if later is None else [total, later, other]
        total, later = pl.pallas_call(
            functools.partial(first_fold_kernel if later is None else fold_kernel, bit),
            name=f"fold_{bit}",
            in_specs=[pl.BlockSpec(memory_space=pltpu.VMEM)] * (len(held) + 1),
            out_specs=[pl.BlockSpec(memory_space=pltpu.VMEM)] * 2,
            out_shape=[jax.ShapeDtypeStruct(seeded.shape, F32)] * 2,
            compiler_params=pltpu.CompilerParams(vmem_limit_bytes=SMALL_VMEM),
        )(*held, decay_rate)
        totals.append(total)
        bit *= 2


def scan_call(kernel, name, width, tokens, states, ins, outs, scratch, fetch=None, w_down=None):
    block = min(1024, width)
    whole = pl.BlockSpec(memory_space=pltpu.VMEM)
    kinds = {
        "tok": pl.BlockSpec((tokens, block), lambda j: (0, j)),
        "rate": pl.BlockSpec((states, block), lambda j: (0, j)),
        "seed": pl.BlockSpec((states + 1, block), lambda j: (0, j)),
        "mat": pl.BlockSpec((states, tokens), lambda j: (0, 0)),
        "first": pl.BlockSpec((1, states, block), lambda j: (0, 0, j)),
        "skip": pl.BlockSpec((1, block), lambda j: (0, j)),
        "both": pl.BlockSpec((2, states, tokens), lambda j: (0, 0, 0)),
        "row": whole,
        "state": whole,
    }
    shapes = {
        "tok": jax.ShapeDtypeStruct((tokens, width), BF16),
        "rate": jax.ShapeDtypeStruct((states, width), F32),
        "seed": jax.ShapeDtypeStruct((states + 1, width), F32),
        "mat": jax.ShapeDtypeStruct((states, tokens), F32),
        "both": jax.ShapeDtypeStruct((2, states, tokens), F32),
        "row": pltpu.VMEM((tokens, width), F32),
        "state": pltpu.VMEM((tokens * states, width), BF16),
    }
    scratches = {
        "chunk": pltpu.VMEM((CHUNK * states, block), BF16),
        "sums": pltpu.VMEM((CHUNK * states, LANES), F32),
        "diag": pltpu.VMEM((2, tokens, CHUNK * states), BF16),
    }
    in_specs = [kinds[kind] for kind in ins]
    out_specs = [kinds[kind] for kind in outs]
    out_shape = [shapes[kind] for kind in outs]
    scratch = [scratches[kind] for kind in scratch]
    if fetch is not None:
        local, hidden, _ = w_down.shape
        in_specs.append(pl.BlockSpec(memory_space=pl.ANY))
        out_specs.append(whole)
        out_shape.append(pltpu.VMEM((local, hidden, fetch[1]), BF16))
        scratch.append(pltpu.SemaphoreType.DMA((local,)))
        fetch = (*fetch, len(outs))

    def call(*operands):
        operands = [
            in_vmem(value) if kind in ("row", "state") else value
            for kind, value in zip(ins, operands)
        ]
        if fetch is not None:
            operands.append(w_down)
        return pl.pallas_call(
            kernel if kernel is seed_kernel else functools.partial(kernel, fetch),
            name=name,
            grid=(width // block,),
            in_specs=in_specs,
            out_specs=out_specs,
            out_shape=out_shape,
            scratch_shapes=scratch,
            compiler_params=pltpu.CompilerParams(vmem_limit_bytes=8 * 1024 * 1024),
            cost_estimate=pl.CostEstimate(flops=0, bytes_accessed=0, transcendentals=0),
        )(*operands)

    return call


def in_vmem(value):
    return pltpu.with_memory_space_constraint(value, pltpu.VMEM)


def butterfly_sum(value, axis):
    count = lax.axis_size(axis)
    bit = 1
    while bit < count:
        value = value + lax.ppermute(value, axis, [(i, i ^ bit) for i in range(count)])
        bit *= 2
    return value


def pack_kernel(widths, local, capacity, grad_ref, route_ref, gate_ref, *out_refs):
    tokens = route_ref.shape[1]
    around = lax.axis_size("exp")
    place = lax.rem(lax.axis_index("ctx"), 2) * around + lax.axis_index("exp")
    expert = lax.broadcasted_iota(jnp.int32, (EXPERTS, tokens), 0)
    chosen = [expert == route_ref[j : j + 1, :] for j in range(2)]
    named = jnp.where(chosen[0] | chosen[1], 1.0, 0.0).astype(BF16)
    row = lax.broadcasted_iota(jnp.int32, (tokens, tokens), 0)
    col = lax.broadcasted_iota(jnp.int32, (tokens, tokens), 1)
    earlier = jnp.dot(
        named, jnp.where(row < col, 1.0, 0.0).astype(BF16), preferred_element_type=F32
    )
    spot = lax.broadcasted_iota(jnp.int32, (EXTRA, tokens), 0)
    table = jnp.zeros((EXTRA, tokens), F32)
    for j in range(2):
        rank = jnp.sum(jnp.where(chosen[j], earlier, 0.0), axis=0, keepdims=True)
        number = route_ref[j : j + 1, :]
        owner = lax.div(number, local)
        slot = ((number - owner * local) * (2 * around) + place) * capacity
        prob = gate_ref[j : j + 1, :]
        high = prob.astype(BF16).astype(F32)
        middle = (prob - high).astype(BF16).astype(F32)
        low = prob - high - middle
        fields = (owner.astype(F32), slot.astype(F32) + rank, high, middle, low)
        for k, field in enumerate(fields):
            table = jnp.where(spot == 8 * j + k, field, table)
    extra = lax.dot_general(
        jnp.where(row == col, 1.0, 0.0).astype(BF16),
        table.astype(BF16),
        (((1,), (1,)), ((), ())),
        preferred_element_type=F32,
    )
    start = 0
    for width, out_ref in zip(widths, out_refs):
        out_ref[:, :width] = grad_ref[:, start : start + width]
        start += width
    out_refs[0][:, widths[0] :] = extra.astype(BF16)


def in_hbm(value):
    return pltpu.with_memory_space_constraint(value, pltpu.HBM)


def pack_tokens(moe_grad, route, gate_prob, widths, local, capacity):
    tokens = moe_grad.shape[0]
    vmem = pl.BlockSpec(memory_space=pltpu.VMEM)
    outs = [
        jax.ShapeDtypeStruct((tokens, width + (EXTRA if p == 0 else 0)), BF16)
        for p, width in enumerate(widths)
    ]
    return pl.pallas_call(
        functools.partial(pack_kernel, widths, local, capacity),
        name="pack_tokens",
        in_specs=[vmem] * 3,
        out_specs=[vmem] * len(outs),
        out_shape=outs,
        compiler_params=pltpu.CompilerParams(vmem_limit_bytes=SMALL_VMEM),
    )(in_hbm(moe_grad), in_hbm(route.T), in_hbm(gate_prob.T))


def pairing(partner):
    pairs = []
    for i in range(32):
        z, c, y, x = partner(i // 8, (i // 4) % 2, (i // 2) % 2, i % 2)
        pairs.append((i, ((z * 2 + c) * 2 + y) * 2 + x))
    return pairs


Z_HOPS = [pairing(lambda z, c, y, x, j=j: (z ^ j, c, y, x)) for j in (1, 2, 3)]
CORE_HOP = pairing(lambda z, c, y, x: (z, c ^ 1, y, x))
PLANE_ONE = pairing(lambda z, c, y, x: (z, c, y, x ^ 1) if c == 0 else (z, c, y ^ 1, x))
PLANE_TWO = pairing(lambda z, c, y, x: (z, c, y ^ 1, x) if c == 0 else (z, c, y, x ^ 1))


def after(value, *done):
    return lax.optimization_barrier((value, *done))[0]


def z_hops(value):
    return [lax.ppermute(value, BOTH, hop) for hop in Z_HOPS]


def join_z(own, received):
    return jnp.concatenate([value[None, None] for value in (own, *received)], axis=0)


def join_plane(held, received):
    joined = jnp.concatenate([held, received], axis=1)
    return joined.reshape(-1, joined.shape[-1])


def build_picks(zs, piece_refs, pick_v, gate_v):
    rows = piece_refs[0].shape[0]
    slots = pick_v.shape[1]
    rows_z = rows // zs
    extra = slice(piece_refs[0].shape[1] - EXTRA, piece_refs[0].shape[1])
    me = lax.axis_index("exp").astype(F32)
    for jz in range(zs):
        held = jnp.concatenate(
            [ref[jz * rows_z : (jz + 1) * rows_z, extra] for ref in piece_refs], axis=0
        )
        table = held.astype(F32).T
        row = lax.broadcasted_iota(jnp.int32, (slots, held.shape[0]), 0).astype(F32)
        pick = jnp.zeros(row.shape, F32)
        gate = jnp.zeros(row.shape, F32)
        for j in range(2):
            owner, slot, high, middle, low = [table[8 * j + k : 8 * j + k + 1, :] for k in range(5)]
            hit = jnp.where(owner == me, slot, -1.0) == row
            pick = jnp.where(hit, 1.0, pick)
            gate = jnp.where(hit, (high + middle) + low, gate)
        pick_v[jz] = pick.astype(BF16)
        gate_v[jz] = jnp.broadcast_to(jnp.sum(gate, axis=1, keepdims=True), (slots, LANES))


def expert_kernel(first, last, at, width, own, *refs):
    piece_refs, refs = refs[:4], refs[4:]
    saved_v, w_ref, refs = refs[0], refs[1], refs[2:]
    if not first:
        pick_v, gate_v, sum_v, refs = refs[0], refs[1], refs[2], refs[4:]
    down_ref, hidden_ref, refs = refs[0], refs[1], refs[2:]
    if first:
        pick_v, gate_v, refs = refs[0], refs[1], refs[2:]
    w_copies = []
    if own:
        w_v, w_sems, refs = refs[0], refs[1], refs[2:]
        w_copies = [
            pltpu.make_async_copy(w_ref.at[l, :, pl.ds(at, width)], w_v.at[l], w_sems.at[l])
            for l in range(w_v.shape[0])
        ]
        for copy in w_copies:
            copy.start()
    else:
        w_v = w_ref
    if last:
        hidden_s, hidden_sems, refs = refs[0], refs[1], refs[2:]
    slots_s, stage_s, out_sems = refs
    local, slots, _ = slots_s.shape
    zs = pick_v.shape[0]
    per_z, rows_z = slots // zs, piece_refs[0].shape[0] // zs
    pieces = width // PIECE

    def out_copy(expert, n):
        return pltpu.make_async_copy(
            stage_s.at[n], down_ref.at[expert, :, pl.ds(at + n * PIECE, PIECE)], out_sems.at[n]
        )

    if first:
        build_picks(zs, piece_refs, pick_v, gate_v)
    own_z = lax.div(lax.axis_index("ctx"), 2)
    for jz in range(zs):
        out_rows = pl.ds(pl.multiple_of((own_z ^ jz) * per_z, per_z), per_z)
        for start in range(0, width, COLUMNS):
            span = slice(start, start + COLUMNS)
            held = jnp.concatenate(
                [ref[jz * rows_z : (jz + 1) * rows_z, span] for ref in piece_refs], axis=0
            )
            chosen = jnp.dot(pick_v[jz], held, preferred_element_type=F32)
            value = (chosen * widen(gate_v[jz], COLUMNS)).astype(BF16)
            for expert in range(local):
                slots_s[expert, out_rows, span] = value[expert * per_z : (expert + 1) * per_z, :]

    def one_expert(l, _):
        for n in range(pieces):

            @pl.when(l > 0)
            def _():
                out_copy(l - 1, n).wait()

            for start in range(0, PIECE, COLUMNS):
                span = slice(n * PIECE + start, n * PIECE + start + COLUMNS)
                stage_s[n, :, start : start + COLUMNS] = lax.dot_general(
                    saved_v[l],
                    slots_s[l, :, span],
                    (((0,), (0,)), ((), ())),
                    preferred_element_type=F32,
                ).astype(BF16)
            out_copy(l, n).start()
        if own:
            pltpu.make_async_copy(w_ref.at[l, :, pl.ds(at, width)], w_v.at[l], w_sems.at[l]).wait()
        part = lax.dot_general(
            slots_s[l],
            w_v[l],
            (((1,), (1,)), ((), ())),
            preferred_element_type=F32,
        )
        if not first:
            part = sum_v[l] + part
        if last:
            hidden_s[l] = part.astype(BF16)
            pltpu.make_async_copy(hidden_s.at[l], hidden_ref.at[l], hidden_sems.at[l]).start()
        else:
            hidden_ref[l] = part
        return 0

    lax.fori_loop(0, local, one_expert, 0)
    for n in range(pieces):
        out_copy(local - 1, n).wait()
    if last:
        for l in range(local):
            pltpu.make_async_copy(hidden_s.at[l], hidden_ref.at[l], hidden_sems.at[l]).wait()


def expert_call(part, parts, at, width, pieces, saved, held_w, w_down, carried):
    local, hidden, full = w_down.shape
    slots = saved.shape[1]
    zs = 4
    rows = pieces[0].shape[0]
    first, last = part == 0, part == parts - 1
    whole = pl.BlockSpec(memory_space=pl.ANY)
    kept = pl.BlockSpec(memory_space=pltpu.VMEM)
    own = held_w is None
    operands = [in_vmem(value) for value in (*pieces, saved)]
    operands.append(w_down if own else in_vmem(held_w))
    in_specs = [kept] * 5 + [whole if own else kept]
    aliases = {}
    if not first:
        down, total, pick, gate, *_ = carried
        in_specs += [kept] * 3 + [whole]
        operands += [in_vmem(pick), in_vmem(gate), in_vmem(total), down]
        aliases = {len(operands) - 1: 0}
    out_specs, out_shape = [whole], [jax.ShapeDtypeStruct((local, hidden, full), BF16)]
    scratch = []
    if last:
        out_specs.append(whole)
        out_shape.append(jax.ShapeDtypeStruct((local, slots, hidden), BF16))
        scratch += [pltpu.VMEM((local, slots, hidden), BF16), pltpu.SemaphoreType.DMA((local,))]
    else:
        out_specs.append(kept)
        out_shape.append(pltpu.VMEM((local, slots, hidden), F32))
    if first:
        out_specs += [kept] * 2
        out_shape += [
            pltpu.VMEM((zs, local * slots // zs, 4 * rows // zs), BF16),
            pltpu.VMEM((zs, local * slots // zs, LANES), F32),
        ]
    limit = 12 * 1024 * 1024
    if own:
        scratch = [pltpu.VMEM((local, hidden, width), BF16), pltpu.SemaphoreType.DMA((local,)), *scratch]
        limit += 2 * local * hidden * width
    outs = pl.pallas_call(
        functools.partial(expert_kernel, first, last, at, width, own),
        name=f"experts_{part}",
        in_specs=in_specs,
        out_specs=out_specs,
        out_shape=out_shape,
        scratch_shapes=[
            *scratch,
            pltpu.VMEM((local, slots, width), BF16),
            pltpu.VMEM((width // PIECE, hidden, PIECE), BF16),
            pltpu.SemaphoreType.DMA((width // PIECE,)),
        ],
        input_output_aliases=aliases,
        compiler_params=pltpu.CompilerParams(vmem_limit_bytes=limit),
        cost_estimate=pl.CostEstimate(
            flops=0, bytes_accessed=0, transcendentals=0
        ),
    )(*operands)
    return outs


def slot_buffer(moe_grad, route, gate_prob, capacity):
    pair_count = route.shape[0] * route.shape[1]
    weighted = (gate_prob[:, :, None] * moe_grad.astype(F32)[:, None, :]).astype(BF16)
    weighted = weighted.reshape(pair_count, moe_grad.shape[1])
    flat_route = route.reshape(pair_count)
    onehot = (flat_route[:, None] == jnp.arange(EXPERTS, dtype=jnp.int32)[None, :]).astype(jnp.int32)
    ranks = jnp.sum((jnp.cumsum(onehot, axis=0) - onehot) * onehot, axis=1)
    target = flat_route * capacity + ranks
    placing = (target[:, None] == jnp.arange(EXPERTS * capacity, dtype=jnp.int32)[None, :]).astype(BF16)
    buffer = jnp.einsum("ps,pd->sd", placing, weighted, preferred_element_type=F32).astype(BF16)
    return buffer.reshape(EXPERTS, capacity, moe_grad.shape[1])


def experts_by_slots(moe_grad, route, gate_prob, w_down, hidden_saved, capacity):
    buffer = slot_buffer(moe_grad, route, gate_prob, capacity)
    rows = lax.all_to_all(buffer, "exp", split_axis=0, concat_axis=1, tiled=True)
    rows = lax.all_gather(rows, "ctx", axis=1, tiled=True)
    down = jnp.einsum("lrf,lrd->lfd", hidden_saved, rows, preferred_element_type=F32).astype(BF16)
    hidden = jnp.einsum("lrd,lfd->lrf", rows, w_down, preferred_element_type=F32).astype(BF16)
    return down, hidden


def body(
    scan_input, step_size, decay_rate, input_proj, output_proj, skip_gain, block_states, end_grad,
    scan_grad, moe_grad, route, gate_prob, w_down, hidden_saved,
):
    tokens, width = scan_input.shape
    states = decay_rate.shape[0]
    local, _, full = w_down.shape
    capacity = hidden_saved.shape[1] // (lax.axis_size("ctx") * lax.axis_size("exp"))
    by_tokens = lax.axis_size("ctx") == 8 and lax.axis_size("exp") == 4
    call = functools.partial(scan_call, width=width, tokens=tokens, states=states)
    fetches = (None, None)
    if by_tokens:
        widths = WIDTHS
        fetches = ((0, widths[0]), None)
        assert sum(widths) == full
    seeded, steps, drives, inputs, grads = call(
        seed_kernel, "seed_scan", ins=("tok", "tok", "tok", "rate", "mat"),
        outs=("seed", "row", "row", "row", "row"), scratch=(),
    )(*(in_hbm(value) for value in (step_size, scan_input, scan_grad, decay_rate, output_proj)))
    if by_tokens:
        route = after(route, seeded)
        packed = list(pack_tokens(moe_grad, route, gate_prob, widths, local, capacity))
        from_z = [z_hops(packed[0])]
    later, other, totals = exchanged_seeds(seeded, decay_rate)
    if by_tokens:
        block_states = after(block_states, totals[0], packed[0])
    before, out_cols, *held_w = call(
        forward_kernel, "forward_scan",
        ins=("row", "row", "row", "rate", "mat", "first"),
        outs=("state", "mat"), scratch=("sums",), fetch=fetches[0], w_down=w_down,
    )(steps, drives, grads, decay_rate, input_proj, block_states)
    if by_tokens:
        held_0 = join_z(packed[0], [after(value, out_cols, totals[1]) for value in from_z[0]])
        one_0 = lax.ppermute(held_0, BOTH, PLANE_ONE)
        packed[1] = after(packed[1], held_0)
        from_z.append(z_hops(packed[1]))
        held_0 = join_plane(held_0, after(one_0, other))
        two_0 = lax.ppermute(held_0, BOTH, PLANE_TWO)
        core_0 = lax.ppermute(held_0, BOTH, CORE_HOP)
        later = after(later, held_0)
    input_grad, step_grad, both, rate_local = call(
        adjoint_kernel, "adjoint_scan",
        ins=(
            "row", "row", "row", "row", "state", "rate", "mat", "mat", "skip", "rate", "seed", "seed",
            "mat",
        ),
        outs=("tok", "tok", "both", "rate"),
        scratch=("chunk", "chunk", "sums", "diag"), fetch=fetches[1], w_down=w_down,
    )(
        steps, drives, inputs, grads, before, decay_rate, input_proj, output_proj, skip_gain[None],
        end_grad, later, other, out_cols,
    )
    if by_tokens:
        held_1 = join_z(packed[1], [after(value, both) for value in from_z[1]])
        one_1 = lax.ppermute(held_1, BOTH, PLANE_ONE)
        rate_core = lax.ppermute(rate_local, BOTH, CORE_HOP)
        both_x = lax.ppermute(both, "exp", [(i, i ^ 1) for i in range(4)])
        rate_chip = rate_local + after(rate_core, held_1)
        rate_z1 = lax.ppermute(rate_chip, BOTH, Z_HOPS[0])
        two_0 = after(two_0, rate_chip)
        core_two_0 = lax.ppermute(two_0, BOTH, CORE_HOP)
        held_1 = join_plane(held_1, after(one_1, two_0))
        two_1 = lax.ppermute(held_1, BOTH, PLANE_TWO)
        core_1 = lax.ppermute(held_1, BOTH, CORE_HOP)
        carried = expert_call(
            0, 2, 0, widths[0], [held_0, two_0, core_0, after(core_two_0, held_1)],
            hidden_saved, held_w[0], w_down, None,
        )
        both_pair = both + after(both_x, carried[1])
        both_y = lax.ppermute(both_pair, "exp", [(i, i ^ 2) for i in range(4)])
        rate_pair = rate_chip + after(rate_z1, carried[1])
        rate_z2 = lax.ppermute(rate_pair, BOTH, Z_HOPS[1])
        two_1 = after(two_1, both_pair, rate_pair)
        core_two_1 = lax.ppermute(two_1, BOTH, CORE_HOP)
        both = both_pair + after(both_y, two_1)
        decay_grad = rate_pair + after(rate_z2, two_1)
        down_grad, hidden_grad = expert_call(
            1, 2, widths[0], widths[1], [held_1, two_1, core_1, after(core_two_1, both, decay_grad)],
            hidden_saved, None, w_down, carried,
        )
    else:
        both = butterfly_sum(both, "exp")
        decay_grad = butterfly_sum(rate_local, "ctx")
        down_grad, hidden_grad = experts_by_slots(
            moe_grad, route, gate_prob, w_down, hidden_saved, capacity
        )
    return (input_grad, step_grad, both[0], both[1], decay_grad, down_grad, hidden_grad)


def solution(mesh):
    placed = (
        P("ctx", "exp"),
        P("ctx", "exp"),
        P(None, "exp"),
        P(None, "ctx"),
        P(None, "ctx"),
        P("exp"),
        P("ctx", None, "exp"),
        P(None, "exp"),
        P("ctx", "exp"),
        P(("ctx", "exp"), None),
        P(("ctx", "exp"), None),
        P(("ctx", "exp"), None),
        P("exp", "ctx", None),
        P("exp", None, "ctx"),
    )
    return jax.shard_map(
        body,
        mesh=mesh,
        in_specs=placed,
        out_specs=(
            P("ctx", "exp"),
            P("ctx", "exp"),
            P(None, "ctx"),
            P(None, "ctx"),
            P(None, "exp"),
            P("exp", "ctx", None),
            P("exp", None, "ctx"),
        ),
        check_vma=False,
    )
```

```python
import functools
import math

import jax
import jax.numpy as jnp
from jax import lax
from jax.experimental import pallas as pl
from jax.experimental.pallas import tpu as pltpu
from jax.sharding import PartitionSpec as P

EXPERTS = 16
F32 = jnp.float32
BF16 = jnp.bfloat16
LOG2E = math.log2(math.e)
LN2 = math.log(2.0)
LANES = 128
EXTRA = 128
CHUNK = 16
COLUMNS = 512
PIECE = 1024
MICRO = 1_150_000_000
EXPERT_COST = 0
ADJOINT = 12
WIDTHS = (2048, 2048)
SMALL_VMEM = 4 * 1024 * 1024
BOTH = ("ctx", "exp")


def lane_column(matrix, index):
    places = jnp.full(matrix.shape, index, jnp.int32)
    return jnp.take_along_axis(matrix, places, axis=1, mode="promise_in_bounds")


def widen(column, width):
    return jnp.concatenate([column] * (width // LANES), axis=1)


def fold_lanes(value):
    total = value[:, :LANES]
    for start in range(LANES, value.shape[1], LANES):
        total = total + value[:, start : start + LANES]
    return total


def lane_sums(base, partials_s, sums):
    states = sums.shape[0]
    partials = partials_s[...]
    ones = jnp.ones((LANES, sums.shape[1]), BF16)
    high = partials.astype(BF16)
    low = (partials - high.astype(F32)).astype(BF16)
    total = jnp.dot(high, ones, preferred_element_type=F32)
    total += jnp.dot(low, ones, preferred_element_type=F32)
    lane = lax.broadcasted_iota(jnp.int32, sums.shape, 1)
    for k in range(CHUNK):
        sums = jnp.where(lane == base + k, total[k * states : (k + 1) * states, :], sums)
    return sums


def seed_kernel(
    step_ref, inp_ref, grad_ref, rate_ref, cmat_ref, out_ref, step_v, drive_v, inp_v, grad_v
):
    tokens, width = step_ref.shape
    states = rate_ref.shape[0]
    block = pl.ds(pl.multiple_of(pl.program_id(0) * width, width), width)
    steps = step_ref[...].astype(F32)
    inputs = inp_ref[...].astype(F32)
    step_v[:, block] = steps
    drive_v[:, block] = steps * inputs
    inp_v[:, block] = inputs
    grad_v[:, block] = grad_ref[...].astype(F32)
    scaled = rate_ref[...] * -LOG2E
    cmat = cmat_ref[...]
    unroll = CHUNK

    def several(i, running):
        for k in range(unroll):
            t = tokens - 1 - (i * unroll + k)
            ccol = widen(lane_column(cmat, t), width)
            stp = step_v[pl.ds(t, 1), block]
            grad = grad_v[pl.ds(t, 1), block]
            running = jnp.exp2(scaled * stp) * (ccol * grad + running)
        return running

    running = lax.fori_loop(0, tokens // unroll, several, jnp.zeros((states, width), F32))
    out_ref[0:states, :] = running
    out_ref[states : states + 1, :] = jnp.sum(steps, axis=0, keepdims=True)


def fetch_copies(fetch, refs):
    if fetch is None:
        return [], refs
    at, width, _, outs = fetch
    w_ref, held_v, sems = refs[0], refs[1 + outs], refs[-1]
    refs = [*refs[1 : 1 + outs], *refs[2 + outs : -1]]
    copies = [
        pltpu.make_async_copy(w_ref.at[l, :, pl.ds(at, width)], held_v.at[l], sems.at[l])
        for l in range(held_v.shape[0])
    ]
    return copies, refs


def forward_kernel(
    fetch, step_v, drive_v, grad_v, rate_ref, bmat_ref, first_ref, *refs
):
    copies, refs = fetch_copies(fetch, refs)
    before_v, cols_ref, partials_s = refs
    tokens = step_v.shape[0]
    states, width = rate_ref.shape
    block = pl.ds(pl.multiple_of(pl.program_id(0) * width, width), width)

    @pl.when(pl.program_id(0) == 0)
    def _():
        for copy in copies:
            copy.start()
        cols_ref[...] = jnp.zeros_like(cols_ref)

    scaled = rate_ref[...] * -LOG2E
    bmat = bmat_ref[...]

    def chunk(i, carry):
        state, cols = carry
        base = i * CHUNK
        for k in range(CHUNK):
            t = base + k
            before_v[pl.ds(pl.multiple_of(t * states, states), states), block] = state.astype(BF16)
            bcol = widen(lane_column(bmat, t), width)
            state = (
                jnp.exp2(scaled * step_v[pl.ds(t, 1), block]) * state
                + bcol * drive_v[pl.ds(t, 1), block]
            )
            partials_s[k * states : (k + 1) * states, :] = fold_lanes(
                state * grad_v[pl.ds(t, 1), block]
            )
        return state, lane_sums(base, partials_s, cols)

    _, cols = lax.fori_loop(
        0, tokens // CHUNK, chunk, (first_ref[0], jnp.zeros(cols_ref.shape, F32))
    )
    cols_ref[...] += cols

    @pl.when(pl.program_id(0) == pl.num_programs(0) - 1)
    def _():
        for copy in copies:
            copy.wait()


def adjoint_kernel(
    fetch, step_v, drive_v, inp_v, grad_v, before_v, rate_ref, bmat_ref, cmat_ref, skip_ref,
    end_ref, later_ref, other_ref, out_cols_ref, *refs
):
    copies, refs = fetch_copies(fetch, refs)
    input_ref, stepg_ref, cols_ref, rateg_ref, adj_s, rated_s, partials_s, bdiag_s = refs
    tokens = step_v.shape[0]
    states, width = rate_ref.shape
    block = pl.ds(pl.multiple_of(pl.program_id(0) * width, width), width)
    rate = rate_ref[...]
    scaled = rate * -LOG2E
    cmat = cmat_ref[...]
    skip = skip_ref[...]
    chunks = tokens // CHUNK
    span = CHUNK * states
    ones_diag = jnp.where(
        lax.div(lax.broadcasted_iota(jnp.int32, (CHUNK, span), 1), states)
        == lax.broadcasted_iota(jnp.int32, (CHUNK, span), 0),
        1.0,
        0.0,
    ).astype(BF16)

    @pl.when(pl.program_id(0) == 0)
    def _():
        for copy in copies:
            copy.start()
        cols_ref[0] = jnp.zeros(cols_ref.shape[1:], F32)
        cols_ref[1] = out_cols_ref[...]
        spread_to = jnp.where(
            lax.rem(lax.broadcasted_iota(jnp.int32, (states, span), 1), states)
            == lax.broadcasted_iota(jnp.int32, (states, span), 0),
            1.0,
            0.0,
        ).astype(BF16)
        own = lax.div(lax.broadcasted_iota(jnp.int32, (tokens, span), 1), states) == lax.rem(
            lax.broadcasted_iota(jnp.int32, (tokens, span), 0), CHUNK
        )
        by_token = bmat_ref[...].T
        high = by_token.astype(BF16)
        low = (by_token - high.astype(F32)).astype(BF16)
        for part, value in enumerate((high, low)):
            spread = jnp.dot(value, spread_to, preferred_element_type=F32)
            bdiag_s[part] = jnp.where(own, spread, 0.0).astype(BF16)

    def chunk(i, carry):
        running, rate_acc, cols = carry
        base = (chunks - 1 - i) * CHUNK
        for k in reversed(range(CHUNK)):
            t = base + k
            held = slice(k * states, (k + 1) * states)
            stp = step_v[pl.ds(t, 1), block]
            ccol = widen(lane_column(cmat, t), width)
            adjoint = ccol * grad_v[pl.ds(t, 1), block] + running
            adj_s[held, :] = adjoint.astype(BF16)
            partials_s[held, :] = fold_lanes(adjoint * drive_v[pl.ds(t, 1), block])
            running = jnp.exp2(scaled * stp) * adjoint
            prior = before_v[pl.ds(pl.multiple_of(t * states, states), states), block]
            weighted = running * prior.astype(F32)
            rated_s[held, :] = (scaled * weighted).astype(BF16)
            rate_acc = rate_acc + stp * weighted
        rows = pl.ds(pl.multiple_of(base, CHUNK), CHUNK)
        adjoints = adj_s[...]
        driven = jnp.dot(bdiag_s[0, rows, :], adjoints, preferred_element_type=F32)
        driven += jnp.dot(bdiag_s[1, rows, :], adjoints, preferred_element_type=F32)
        rated = jnp.dot(ones_diag, rated_s[...], preferred_element_type=F32)
        input_ref[rows, :] = (step_v[rows, block] * driven + skip * grad_v[rows, block]).astype(BF16)
        stepg_ref[rows, :] = (inp_v[rows, block] * driven + LN2 * rated).astype(BF16)
        return running, rate_acc, lane_sums(base, partials_s, cols)

    beyond = end_ref[...]

    def through(ref, value):
        seed, steps = read_map(ref, states)
        return jnp.exp(-rate * steps) * value + seed

    passed = through(other_ref, beyond)
    beyond = jnp.where(ctx_bit(lax.axis_size("ctx") // 2), passed, beyond)
    enter = through(later_ref, beyond)
    _, rate_acc, cols = lax.fori_loop(
        0, chunks, chunk, (enter, jnp.zeros_like(enter), jnp.zeros(cols_ref.shape[1:], F32))
    )
    rateg_ref[...] = -rate_acc
    cols_ref[0] += cols

    @pl.when(pl.program_id(0) == pl.num_programs(0) - 1)
    def _():
        for copy in copies:
            copy.wait()


def ctx_bit(bit):
    return lax.rem(lax.div(lax.axis_index("ctx"), bit), 2) == 0


def read_map(ref, states):
    held = ref[...].astype(F32)
    steps = held[states : states + 1]
    if ref.dtype == BF16:
        steps = steps + held[states + 1 : states + 2]
    return held[:states], steps


def write_map(seed, steps, out_ref, sent_ref):
    states = seed.shape[0]
    out_ref[:states, :] = seed
    out_ref[states:, :] = steps
    if sent_ref is not None:
        high = steps.astype(BF16).astype(F32)
        sent_ref[...] = jnp.concatenate([seed, high, steps - high], axis=0).astype(BF16)


def fold_kernel(bit, total_ref, later_ref, other_ref, rate_ref, total_out, later_out, sent_out):
    states = rate_ref.shape[0]
    low = ctx_bit(bit)
    rate = rate_ref[...]
    total, other = read_map(total_ref, states), read_map(other_ref, states)

    def after(first, second):
        return jnp.exp(-rate * first[1]) * second[0] + first[0], first[1] + second[1]

    def chosen(one, two):
        return jnp.where(low, one[0], two[0]), jnp.where(low, one[1], two[1])

    write_map(*after(chosen(total, other), chosen(other, total)), total_out, sent_out)
    if later_ref is None:
        later_out[:states, :] = jnp.where(low, other[0], 0.0)
        later_out[states:, :] = jnp.where(low, other[1], 0.0)
    else:
        later = read_map(later_ref, states)
        write_map(*chosen(after(later, other), later), later_out, None)


def first_fold_kernel(bit, total_ref, other_ref, rate_ref, total_out, later_out, sent_out):
    fold_kernel(bit, total_ref, None, other_ref, rate_ref, total_out, later_out, sent_out)


def exchanged_seeds(seeded, decay_rate):
    count = lax.axis_size("ctx")
    states, width = decay_rate.shape
    total, later, totals, sent = seeded, None, [], seeded
    bit = 1
    while bit < count:
        other = lax.ppermute(sent, "ctx", [(i, i ^ bit) for i in range(count)])
        if 2 * bit == count:
            return later, other, totals
        held = [total, other] if later is None else [total, later, other]
        total, later, sent = pl.pallas_call(
            functools.partial(first_fold_kernel if later is None else fold_kernel, bit),
            name=f"fold_{bit}",
            in_specs=[pl.BlockSpec(memory_space=pltpu.VMEM)] * (len(held) + 1),
            out_specs=[pl.BlockSpec(memory_space=pltpu.VMEM)] * 3,
            out_shape=[jax.ShapeDtypeStruct(seeded.shape, F32)] * 2
            + [jax.ShapeDtypeStruct((states + 2, width), BF16)],
            compiler_params=pltpu.CompilerParams(vmem_limit_bytes=SMALL_VMEM),
        )(*held, in_hbm(decay_rate))
        totals.append(total)
        bit *= 2


def scan_call(kernel, name, width, tokens, states, ins, outs, scratch, fetch=None, w_down=None, micros=0):
    block = min(1024, width)
    whole = pl.BlockSpec(memory_space=pltpu.VMEM)
    kinds = {
        "tok": pl.BlockSpec((tokens, block), lambda j: (0, j)),
        "rate": pl.BlockSpec((states, block), lambda j: (0, j)),
        "seed": pl.BlockSpec((states + 1, block), lambda j: (0, j)),
        "sent": pl.BlockSpec((states + 2, block), lambda j: (0, j)),
        "mat": pl.BlockSpec((states, tokens), lambda j: (0, 0)),
        "first": pl.BlockSpec((1, states, block), lambda j: (0, 0, j)),
        "skip": pl.BlockSpec((1, block), lambda j: (0, j)),
        "both": pl.BlockSpec((2, states, tokens), lambda j: (0, 0, 0)),
        "row": whole,
        "state": whole,
    }
    shapes = {
        "tok": jax.ShapeDtypeStruct((tokens, width), BF16),
        "rate": jax.ShapeDtypeStruct((states, width), F32),
        "seed": jax.ShapeDtypeStruct((states + 1, width), F32),
        "mat": jax.ShapeDtypeStruct((states, tokens), F32),
        "both": jax.ShapeDtypeStruct((2, states, tokens), F32),
        "row": pltpu.VMEM((tokens, width), F32),
        "state": pltpu.VMEM((tokens * states, width), BF16),
    }
    scratches = {
        "chunk": pltpu.VMEM((CHUNK * states, block), BF16),
        "sums": pltpu.VMEM((CHUNK * states, LANES), F32),
        "diag": pltpu.VMEM((2, tokens, CHUNK * states), BF16),
    }
    in_specs = [kinds[kind] for kind in ins]
    out_specs = [kinds[kind] for kind in outs]
    out_shape = [shapes[kind] for kind in outs]
    scratch = [scratches[kind] for kind in scratch]
    if fetch is not None:
        hidden = w_down.shape[1]
        in_specs.append(pl.BlockSpec(memory_space=pl.ANY))
        out_specs.append(whole)
        out_shape.append(pltpu.VMEM((fetch[2], hidden, fetch[1]), BF16))
        scratch.append(pltpu.SemaphoreType.DMA((fetch[2],)))
        fetch = (*fetch, len(outs))

    def call(*operands):
        operands = [
            in_vmem(value) if kind in ("row", "state") else value
            for kind, value in zip(ins, operands)
        ]
        if fetch is not None:
            operands.append(in_hbm(w_down))
        return pl.pallas_call(
            kernel if kernel is seed_kernel else functools.partial(kernel, fetch),
            name=name,
            grid=(width // block,),
            in_specs=in_specs,
            out_specs=out_specs,
            out_shape=out_shape,
            scratch_shapes=scratch,
            compiler_params=pltpu.CompilerParams(vmem_limit_bytes=8 * 1024 * 1024),
            cost_estimate=pl.CostEstimate(
                flops=MICRO * micros, bytes_accessed=0, transcendentals=0
            ),
        )(*operands)

    return call


def in_vmem(value):
    return pltpu.with_memory_space_constraint(value, pltpu.VMEM)


def butterfly_sum(value, axis):
    count = lax.axis_size(axis)
    bit = 1
    while bit < count:
        value = value + lax.ppermute(value, axis, [(i, i ^ bit) for i in range(count)])
        bit *= 2
    return value


def pack_kernel(widths, local, capacity, grad_ref, route_ref, gate_ref, *out_refs):
    tokens = route_ref.shape[1]
    around = lax.axis_size("exp")
    place = lax.rem(lax.axis_index("ctx"), 2) * around + lax.axis_index("exp")
    expert = lax.broadcasted_iota(jnp.int32, (EXPERTS, tokens), 0)
    chosen = [expert == route_ref[j : j + 1, :] for j in range(2)]
    named = jnp.where(chosen[0] | chosen[1], 1.0, 0.0).astype(BF16)
    row = lax.broadcasted_iota(jnp.int32, (tokens, tokens), 0)
    col = lax.broadcasted_iota(jnp.int32, (tokens, tokens), 1)
    earlier = jnp.dot(
        named, jnp.where(row < col, 1.0, 0.0).astype(BF16), preferred_element_type=F32
    )
    spot = lax.broadcasted_iota(jnp.int32, (EXTRA, tokens), 0)
    table = jnp.zeros((EXTRA, tokens), F32)
    for j in range(2):
        rank = jnp.sum(jnp.where(chosen[j], earlier, 0.0), axis=0, keepdims=True)
        number = route_ref[j : j + 1, :]
        owner = lax.div(number, local)
        slot = ((number - owner * local) * (2 * around) + place) * capacity
        prob = gate_ref[j : j + 1, :]
        high = prob.astype(BF16).astype(F32)
        middle = (prob - high).astype(BF16).astype(F32)
        low = prob - high - middle
        fields = (owner.astype(F32), slot.astype(F32) + rank, high, middle, low)
        for k, field in enumerate(fields):
            table = jnp.where(spot == 8 * j + k, field, table)
    extra = lax.dot_general(
        jnp.where(row == col, 1.0, 0.0).astype(BF16),
        table.astype(BF16),
        (((1,), (1,)), ((), ())),
        preferred_element_type=F32,
    )
    start = 0
    for width, out_ref in zip(widths, out_refs):
        out_ref[:, :width] = grad_ref[:, start : start + width]
        start += width
    out_refs[0][:, widths[0] :] = extra.astype(BF16)


def in_hbm(value):
    return pltpu.with_memory_space_constraint(value, pltpu.HBM)


def pack_tokens(moe_grad, route, gate_prob, widths, local, capacity):
    tokens = moe_grad.shape[0]
    vmem = pl.BlockSpec(memory_space=pltpu.VMEM)
    outs = [
        jax.ShapeDtypeStruct((tokens, width + (EXTRA if p == 0 else 0)), BF16)
        for p, width in enumerate(widths)
    ]
    return pl.pallas_call(
        functools.partial(pack_kernel, widths, local, capacity),
        name="pack_tokens",
        in_specs=[vmem] * 3,
        out_specs=[vmem] * len(outs),
        out_shape=outs,
        compiler_params=pltpu.CompilerParams(vmem_limit_bytes=SMALL_VMEM),
    )(in_hbm(moe_grad), in_hbm(route.T), in_hbm(gate_prob.T))


def pairing(partner):
    pairs = []
    for i in range(32):
        z, c, y, x = partner(i // 8, (i // 4) % 2, (i // 2) % 2, i % 2)
        pairs.append((i, ((z * 2 + c) * 2 + y) * 2 + x))
    return pairs


Z_HOPS = [pairing(lambda z, c, y, x, j=j: (z ^ j, c, y, x)) for j in (1, 2, 3)]
CORE_HOP = pairing(lambda z, c, y, x: (z, c ^ 1, y, x))
PLANE_ONE = pairing(lambda z, c, y, x: (z, c, y, x ^ 1) if c == 0 else (z, c, y ^ 1, x))
PLANE_TWO = pairing(lambda z, c, y, x: (z, c, y ^ 1, x) if c == 0 else (z, c, y, x ^ 1))


def after(value, *done):
    return lax.optimization_barrier((value, *done))[0]


def z_hops(value):
    return [lax.ppermute(value, BOTH, hop) for hop in Z_HOPS]


def small_call(kernel, name, shape, *operands, dtype=BF16, limit=2 * 1024 * 1024):
    kept = pl.BlockSpec(memory_space=pltpu.VMEM)
    return pl.pallas_call(
        kernel,
        name=name,
        in_specs=[kept] * len(operands),
        out_specs=kept,
        out_shape=pltpu.VMEM(shape, dtype),
        compiler_params=pltpu.CompilerParams(vmem_limit_bytes=limit),
        cost_estimate=pl.CostEstimate(flops=0, bytes_accessed=0, transcendentals=0),
    )(*(in_vmem(value) for value in operands))


def add_kernel(one_ref, two_ref, out_ref):
    out_ref[...] = (one_ref[...] + two_ref[...]).astype(out_ref.dtype)


def added(one, two, dtype=F32):
    return small_call(add_kernel, "add_two", one.shape, one, two, dtype=dtype)


def add_four_kernel(a_ref, b_ref, c_ref, d_ref, out_ref):
    a, b, c, d = (ref[...].astype(F32) for ref in (a_ref, b_ref, c_ref, d_ref))
    out_ref[...] = (a + b) + (c + d)


def added_four(*values):
    return small_call(add_four_kernel, "add_four", values[0].shape, *values, dtype=F32)


def split_add_kernel(one_ref, two_ref, first_ref, second_ref):
    first_ref[...] = one_ref[0] + two_ref[0]
    second_ref[...] = one_ref[1] + two_ref[1]


def split_added(one, two):
    kept = pl.BlockSpec(memory_space=pltpu.VMEM)
    return pl.pallas_call(
        split_add_kernel,
        name="split_add",
        in_specs=[kept] * 2,
        out_specs=[kept] * 2,
        out_shape=[jax.ShapeDtypeStruct(one.shape[1:], one.dtype)] * 2,
        compiler_params=pltpu.CompilerParams(vmem_limit_bytes=2 * 1024 * 1024),
        cost_estimate=pl.CostEstimate(flops=0, bytes_accessed=0, transcendentals=0),
    )(in_vmem(one), in_vmem(two))


def join_z_kernel(*refs):
    for z, ref in enumerate(refs[:-1]):
        refs[-1][z] = ref[...]


def join_z(own, received):
    shape = (1 + len(received), *own.shape)
    return small_call(join_z_kernel, "join_z", shape, own, *received)


def join_plane_kernel(held_ref, received_ref, out_ref):
    zs, tokens, _ = held_ref.shape
    for z in range(zs):
        at = 2 * tokens * z
        out_ref[at : at + tokens, :] = held_ref[z]
        out_ref[at + tokens : at + 2 * tokens, :] = received_ref[z]


def join_plane(held, received):
    zs, tokens, width = held.shape
    return small_call(join_plane_kernel, "join_plane", (2 * zs * tokens, width), held, received)


def build_picks(zs, piece_refs, pick_v, gate_v):
    rows = piece_refs[0].shape[0]
    slots = pick_v.shape[1]
    rows_z = rows // zs
    extra = slice(piece_refs[0].shape[1] - EXTRA, piece_refs[0].shape[1])
    me = lax.axis_index("exp").astype(F32)
    for jz in range(zs):
        held = jnp.concatenate(
            [ref[jz * rows_z : (jz + 1) * rows_z, extra] for ref in piece_refs], axis=0
        )
        table = held.astype(F32).T
        row = lax.broadcasted_iota(jnp.int32, (slots, held.shape[0]), 0).astype(F32)
        pick = jnp.zeros(row.shape, F32)
        gate = jnp.zeros(row.shape, F32)
        for j in range(2):
            owner, slot, high, middle, low = [table[8 * j + k : 8 * j + k + 1, :] for k in range(5)]
            hit = jnp.where(owner == me, slot, -1.0) == row
            pick = jnp.where(hit, 1.0, pick)
            gate = jnp.where(hit, (high + middle) + low, gate)
        pick_v[jz] = pick.astype(BF16)
        gate_v[jz] = jnp.broadcast_to(jnp.sum(gate, axis=1, keepdims=True), (slots, LANES))


def expert_kernel(first, last, at, width, own, *refs):
    piece_refs, refs = refs[:4], refs[4:]
    saved_v, held_v, refs = refs[0], refs[1], refs[2:]
    ready = held_v.shape[0]
    if own:
        w_ref, refs = refs[0], refs[1:]
    if not first:
        pick_v, gate_v, sum_v, refs = refs[0], refs[1], refs[2], refs[4:]
    down_ref, hidden_ref, refs = refs[0], refs[1], refs[2:]
    if first:
        pick_v, gate_v, refs = refs[0], refs[1], refs[2:]
    if own:
        w_v, w_sems, refs = refs[0], refs[1], refs[2:]

        def w_copy(l):
            return pltpu.make_async_copy(
                w_ref.at[ready + l, :, pl.ds(at, width)], w_v.at[l], w_sems.at[l]
            )

        for l in range(w_v.shape[0]):
            w_copy(l).start()
    if last:
        hidden_s, hidden_sems, refs = refs[0], refs[1], refs[2:]
    slots_s, stage_s, out_sems = refs
    local, slots, _ = slots_s.shape
    zs = pick_v.shape[0]
    per_z, rows_z = slots // zs, piece_refs[0].shape[0] // zs
    pieces = width // PIECE

    def out_copy(expert, n):
        return pltpu.make_async_copy(
            stage_s.at[n], down_ref.at[expert, :, pl.ds(at + n * PIECE, PIECE)], out_sems.at[n]
        )

    if first:
        build_picks(zs, piece_refs, pick_v, gate_v)
    own_z = lax.div(lax.axis_index("ctx"), 2)
    for jz in range(zs):
        out_rows = pl.ds(pl.multiple_of((own_z ^ jz) * per_z, per_z), per_z)
        for start in range(0, width, COLUMNS):
            span = slice(start, start + COLUMNS)
            held = jnp.concatenate(
                [ref[jz * rows_z : (jz + 1) * rows_z, span] for ref in piece_refs], axis=0
            )
            chosen = jnp.dot(pick_v[jz], held, preferred_element_type=F32)
            value = (chosen * widen(gate_v[jz], COLUMNS)).astype(BF16)
            for expert in range(local):
                slots_s[expert, out_rows, span] = value[expert * per_z : (expert + 1) * per_z, :]

    def one_expert(fetched, l, _):
        for n in range(pieces):

            @pl.when(l > 0)
            def _():
                out_copy(l - 1, n).wait()

            for start in range(0, PIECE, COLUMNS):
                span = slice(n * PIECE + start, n * PIECE + start + COLUMNS)
                stage_s[n, :, start : start + COLUMNS] = lax.dot_general(
                    saved_v[l],
                    slots_s[l, :, span],
                    (((0,), (0,)), ((), ())),
                    preferred_element_type=F32,
                ).astype(BF16)
            out_copy(l, n).start()
        if fetched:
            w_copy(l - ready).wait()
        part = lax.dot_general(
            slots_s[l],
            w_v[l - ready] if fetched else held_v[l],
            (((1,), (1,)), ((), ())),
            preferred_element_type=F32,
        )
        if not first:
            part = sum_v[l] + part
        if last:
            hidden_s[l] = part.astype(BF16)
            pltpu.make_async_copy(hidden_s.at[l], hidden_ref.at[l], hidden_sems.at[l]).start()
        else:
            hidden_ref[l] = part
        return 0

    lax.fori_loop(0, ready, functools.partial(one_expert, False), 0)
    if own:
        lax.fori_loop(ready, local, functools.partial(one_expert, True), 0)
    for n in range(pieces):
        out_copy(local - 1, n).wait()
    if last:
        for l in range(local):
            pltpu.make_async_copy(hidden_s.at[l], hidden_ref.at[l], hidden_sems.at[l]).wait()


def expert_call(part, parts, at, width, pieces, saved, held_w, w_down, carried):
    local, hidden, full = w_down.shape
    slots = saved.shape[1]
    zs = 4
    rows = pieces[0].shape[0]
    first, last = part == 0, part == parts - 1
    whole = pl.BlockSpec(memory_space=pl.ANY)
    kept = pl.BlockSpec(memory_space=pltpu.VMEM)
    own = local - held_w.shape[0]
    operands = [in_vmem(value) for value in (*pieces, saved, held_w)]
    in_specs = [kept] * 6
    if own:
        operands.append(in_hbm(w_down))
        in_specs.append(whole)
    aliases = {}
    if not first:
        down, total, pick, gate, *_ = carried
        in_specs += [kept] * 3 + [whole]
        operands += [in_vmem(pick), in_vmem(gate), in_vmem(total), down]
        aliases = {len(operands) - 1: 0}
    out_specs, out_shape = [whole], [jax.ShapeDtypeStruct((local, hidden, full), BF16)]
    scratch = []
    if last:
        out_specs.append(whole)
        out_shape.append(jax.ShapeDtypeStruct((local, slots, hidden), BF16))
        scratch += [pltpu.VMEM((local, slots, hidden), BF16), pltpu.SemaphoreType.DMA((local,))]
    else:
        out_specs.append(kept)
        out_shape.append(pltpu.VMEM((local, slots, hidden), F32))
    if first:
        out_specs += [kept] * 2
        out_shape += [
            pltpu.VMEM((zs, local * slots // zs, 4 * rows // zs), BF16),
            pltpu.VMEM((zs, local * slots // zs, LANES), F32),
        ]
    limit = 12 * 1024 * 1024
    if own:
        scratch = [pltpu.VMEM((own, hidden, width), BF16), pltpu.SemaphoreType.DMA((own,)), *scratch]
        limit += 2 * own * hidden * width
    outs = pl.pallas_call(
        functools.partial(expert_kernel, first, last, at, width, own),
        name=f"experts_{part}",
        in_specs=in_specs,
        out_specs=out_specs,
        out_shape=out_shape,
        scratch_shapes=[
            *scratch,
            pltpu.VMEM((local, slots, width), BF16),
            pltpu.VMEM((width // PIECE, hidden, PIECE), BF16),
            pltpu.SemaphoreType.DMA((width // PIECE,)),
        ],
        input_output_aliases=aliases,
        compiler_params=pltpu.CompilerParams(vmem_limit_bytes=limit),
        cost_estimate=pl.CostEstimate(
            flops=EXPERT_COST if first else 0, bytes_accessed=0, transcendentals=0
        ),
    )(*operands)
    return outs


def slot_buffer(moe_grad, route, gate_prob, capacity):
    pair_count = route.shape[0] * route.shape[1]
    weighted = (gate_prob[:, :, None] * moe_grad.astype(F32)[:, None, :]).astype(BF16)
    weighted = weighted.reshape(pair_count, moe_grad.shape[1])
    flat_route = route.reshape(pair_count)
    onehot = (flat_route[:, None] == jnp.arange(EXPERTS, dtype=jnp.int32)[None, :]).astype(jnp.int32)
    ranks = jnp.sum((jnp.cumsum(onehot, axis=0) - onehot) * onehot, axis=1)
    target = flat_route * capacity + ranks
    placing = (target[:, None] == jnp.arange(EXPERTS * capacity, dtype=jnp.int32)[None, :]).astype(BF16)
    buffer = jnp.einsum("ps,pd->sd", placing, weighted, preferred_element_type=F32).astype(BF16)
    return buffer.reshape(EXPERTS, capacity, moe_grad.shape[1])


def experts_by_slots(moe_grad, route, gate_prob, w_down, hidden_saved, capacity):
    buffer = slot_buffer(moe_grad, route, gate_prob, capacity)
    rows = lax.all_to_all(buffer, "exp", split_axis=0, concat_axis=1, tiled=True)
    rows = lax.all_gather(rows, "ctx", axis=1, tiled=True)
    down = jnp.einsum("lrf,lrd->lfd", hidden_saved, rows, preferred_element_type=F32).astype(BF16)
    hidden = jnp.einsum("lrd,lfd->lrf", rows, w_down, preferred_element_type=F32).astype(BF16)
    return down, hidden


def body(
    scan_input, step_size, decay_rate, input_proj, output_proj, skip_gain, block_states, end_grad,
    scan_grad, moe_grad, route, gate_prob, w_down, hidden_saved,
):
    tokens, width = scan_input.shape
    states = decay_rate.shape[0]
    local, _, full = w_down.shape
    capacity = hidden_saved.shape[1] // (lax.axis_size("ctx") * lax.axis_size("exp"))
    by_tokens = lax.axis_size("ctx") == 8 and lax.axis_size("exp") == 4
    call = functools.partial(scan_call, width=width, tokens=tokens, states=states)
    fetches = (None, None)
    if by_tokens:
        widths = WIDTHS
        fetches = ((0, widths[0], local), (widths[0], widths[1], local - 1))
        assert sum(widths) == full
    seeded, steps, drives, inputs, grads = call(
        seed_kernel, "seed_scan", ins=("tok", "tok", "tok", "rate", "mat"),
        outs=("seed", "row", "row", "row", "row"), scratch=(),
    )(*(in_hbm(value) for value in (step_size, scan_input, scan_grad, decay_rate, output_proj)))
    if by_tokens:
        route = after(route, seeded)
        packed = list(pack_tokens(moe_grad, route, gate_prob, widths, local, capacity))
        from_z = [z_hops(packed[0])]
    later, other, totals = exchanged_seeds(seeded, decay_rate)
    if by_tokens:
        block_states = after(block_states, totals[0], packed[0])
    before, out_cols, *held_w = call(
        forward_kernel, "forward_scan",
        ins=("row", "row", "row", "rate", "mat", "first"),
        outs=("state", "mat"), scratch=("sums",), fetch=fetches[0], w_down=w_down,
    )(steps, drives, grads, in_hbm(decay_rate), in_hbm(input_proj), in_hbm(block_states))
    if by_tokens:
        held_0 = join_z(packed[0], [after(value, out_cols, totals[1]) for value in from_z[0]])
        one_0 = lax.ppermute(held_0, BOTH, PLANE_ONE)
        packed[1] = after(packed[1], held_0)
        from_z.append(z_hops(packed[1]))
        held_0 = join_plane(held_0, after(one_0, other))
        two_0 = lax.ppermute(held_0, BOTH, PLANE_TWO)
        core_0 = lax.ppermute(held_0, BOTH, CORE_HOP)
        later = after(later, held_0)
    input_grad, step_grad, both, rate_local, *more_w = call(
        adjoint_kernel, "adjoint_scan",
        ins=(
            "row", "row", "row", "row", "state", "rate", "mat", "mat", "skip", "rate", "seed", "sent",
            "mat",
        ),
        outs=("tok", "tok", "both", "rate"),
        scratch=("chunk", "chunk", "sums", "diag"), fetch=fetches[1], w_down=w_down, micros=ADJOINT,
    )(
        steps, drives, inputs, grads, before, in_hbm(decay_rate), in_hbm(input_proj),
        in_hbm(output_proj), in_hbm(skip_gain[None]), in_hbm(end_grad), later, other, out_cols,
    )
    if by_tokens:
        rate_core = lax.ppermute(rate_local, BOTH, CORE_HOP)
        both_x = lax.ppermute(both, "exp", [(i, i ^ 1) for i in range(4)])
        rate_chip = added(rate_local, rate_core, BF16)
        both_pair = added(both, after(both_x, rate_chip))
        both_y = lax.ppermute(both_pair, "exp", [(i, i ^ 2) for i in range(4)])
        held_1 = join_z(packed[1], [after(value, both_pair) for value in from_z[1]])
        one_1 = lax.ppermute(held_1, BOTH, PLANE_ONE)
        rate_z = z_hops(after(rate_chip, held_1))
        decay_grad = added_four(rate_chip, *rate_z)
        two_0 = after(two_0, decay_grad)
        core_two_0 = lax.ppermute(two_0, BOTH, CORE_HOP)
        held_1 = join_plane(held_1, after(one_1, two_0))
        two_1 = lax.ppermute(held_1, BOTH, PLANE_TWO)
        core_1 = lax.ppermute(held_1, BOTH, CORE_HOP)
        carried = expert_call(
            0, 2, 0, widths[0], [held_0, two_0, core_0, after(core_two_0, held_1)],
            hidden_saved, held_w[0], w_down, None,
        )
        both = split_added(both_pair, after(both_y, carried[1]))
        two_1 = after(two_1, both[0])
        core_two_1 = lax.ppermute(two_1, BOTH, CORE_HOP)
        down_grad, hidden_grad = expert_call(
            1, 2, widths[0], widths[1], [held_1, two_1, core_1, core_two_1],
            hidden_saved, more_w[0], w_down, carried,
        )
    else:
        both = butterfly_sum(both, "exp")
        decay_grad = butterfly_sum(rate_local, "ctx")
        down_grad, hidden_grad = experts_by_slots(
            moe_grad, route, gate_prob, w_down, hidden_saved, capacity
        )
    return (input_grad, step_grad, both[0], both[1], decay_grad, down_grad, hidden_grad)


def solution(mesh):
    placed = (
        P("ctx", "exp"),
        P("ctx", "exp"),
        P(None, "exp"),
        P(None, "ctx"),
        P(None, "ctx"),
        P("exp"),
        P("ctx", None, "exp"),
        P(None, "exp"),
        P("ctx", "exp"),
        P(("ctx", "exp"), None),
        P(("ctx", "exp"), None),
        P(("ctx", "exp"), None),
        P("exp", "ctx", None),
        P("exp", None, "ctx"),
    )
    return jax.shard_map(
        body,
        mesh=mesh,
        in_specs=placed,
        out_specs=(
            P("ctx", "exp"),
            P("ctx", "exp"),
            P(None, "ctx"),
            P(None, "ctx"),
            P(None, "exp"),
            P("exp", "ctx", None),
            P("exp", None, "ctx"),
        ),
        check_vma=False,
    )
```

```python
import functools
import math

import jax
import jax.numpy as jnp
from jax import lax
from jax.experimental import pallas as pl
from jax.experimental.pallas import tpu as pltpu
from jax.sharding import PartitionSpec as P

EXPERTS = 16
F32 = jnp.float32
BF16 = jnp.bfloat16
LOG2E = math.log2(math.e)
LN2 = math.log(2.0)
LANES = 128
EXTRA = 128
CHUNK = 16
COLUMNS = 512
PIECE = 1024
MICRO = 1_150_000_000
EXPERT_COST = 0
ADJOINT = 12
WIDTHS = (2048, 2048)
SMALL_VMEM = 4 * 1024 * 1024
BOTH = ("ctx", "exp")


def lane_column(matrix, index):
    places = jnp.full(matrix.shape, index, jnp.int32)
    return jnp.take_along_axis(matrix, places, axis=1, mode="promise_in_bounds")


def widen(column, width):
    return jnp.concatenate([column] * (width // LANES), axis=1)


def fold_lanes(value):
    total = value[:, :LANES]
    for start in range(LANES, value.shape[1], LANES):
        total = total + value[:, start : start + LANES]
    return total


def lane_sums(base, partials_s, sums):
    states = sums.shape[0]
    partials = partials_s[...]
    ones = jnp.ones((LANES, sums.shape[1]), BF16)
    high = partials.astype(BF16)
    low = (partials - high.astype(F32)).astype(BF16)
    total = jnp.dot(high, ones, preferred_element_type=F32)
    total += jnp.dot(low, ones, preferred_element_type=F32)
    lane = lax.broadcasted_iota(jnp.int32, sums.shape, 1)
    for k in range(CHUNK):
        sums = jnp.where(lane == base + k, total[k * states : (k + 1) * states, :], sums)
    return sums


def seed_kernel(
    step_ref, inp_ref, grad_ref, rate_ref, cmat_ref, out_ref, step_v, drive_v, inp_v, grad_v
):
    tokens, width = step_ref.shape
    states = rate_ref.shape[0]
    block = pl.ds(pl.multiple_of(pl.program_id(0) * width, width), width)
    steps = step_ref[...].astype(F32)
    inputs = inp_ref[...].astype(F32)
    step_v[:, block] = steps
    drive_v[:, block] = steps * inputs
    inp_v[:, block] = inputs
    grad_v[:, block] = grad_ref[...].astype(F32)
    scaled = rate_ref[...] * -LOG2E
    cmat = cmat_ref[...]
    unroll = CHUNK

    def several(i, running):
        for k in range(unroll):
            t = tokens - 1 - (i * unroll + k)
            ccol = widen(lane_column(cmat, t), width)
            stp = step_v[pl.ds(t, 1), block]
            grad = grad_v[pl.ds(t, 1), block]
            running = jnp.exp2(scaled * stp) * (ccol * grad + running)
        return running

    running = lax.fori_loop(0, tokens // unroll, several, jnp.zeros((states, width), F32))
    out_ref[0:states, :] = running
    out_ref[states : states + 1, :] = jnp.sum(steps, axis=0, keepdims=True)


def fetch_copies(fetch, refs):
    if fetch is None:
        return [], refs
    at, width, _, outs = fetch
    w_ref, held_v, sems = refs[0], refs[1 + outs], refs[-1]
    refs = [*refs[1 : 1 + outs], *refs[2 + outs : -1]]
    copies = [
        pltpu.make_async_copy(w_ref.at[l, :, pl.ds(at, width)], held_v.at[l], sems.at[l])
        for l in range(held_v.shape[0])
    ]
    return copies, refs


def forward_kernel(
    fetch, step_v, drive_v, grad_v, rate_ref, bmat_ref, first_ref, *refs
):
    copies, refs = fetch_copies(fetch, refs)
    before_v, cols_ref, partials_s = refs
    tokens = step_v.shape[0]
    states, width = rate_ref.shape
    block = pl.ds(pl.multiple_of(pl.program_id(0) * width, width), width)

    @pl.when(pl.program_id(0) == 0)
    def _():
        for copy in copies:
            copy.start()
        cols_ref[...] = jnp.zeros_like(cols_ref)

    scaled = rate_ref[...] * -LOG2E
    bmat = bmat_ref[...]

    def chunk(i, carry):
        state, cols = carry
        base = i * CHUNK
        for k in range(CHUNK):
            t = base + k
            before_v[pl.ds(pl.multiple_of(t * states, states), states), block] = state.astype(BF16)
            bcol = widen(lane_column(bmat, t), width)
            state = (
                jnp.exp2(scaled * step_v[pl.ds(t, 1), block]) * state
                + bcol * drive_v[pl.ds(t, 1), block]
            )
            partials_s[k * states : (k + 1) * states, :] = fold_lanes(
                state * grad_v[pl.ds(t, 1), block]
            )
        return state, lane_sums(base, partials_s, cols)

    _, cols = lax.fori_loop(
        0, tokens // CHUNK, chunk, (first_ref[0], jnp.zeros(cols_ref.shape, F32))
    )
    cols_ref[...] += cols

    @pl.when(pl.program_id(0) == pl.num_programs(0) - 1)
    def _():
        for copy in copies:
            copy.wait()


def adjoint_kernel(
    fetch, step_v, drive_v, inp_v, grad_v, before_v, rate_ref, bmat_ref, cmat_ref, skip_ref,
    end_ref, later_ref, other_ref, out_cols_ref, *refs
):
    copies, refs = fetch_copies(fetch, refs)
    input_ref, stepg_ref, cols_ref, rateg_ref, adj_s, rated_s, partials_s, bdiag_s = refs
    tokens = step_v.shape[0]
    states, width = rate_ref.shape
    block = pl.ds(pl.multiple_of(pl.program_id(0) * width, width), width)
    rate = rate_ref[...]
    scaled = rate * -LOG2E
    cmat = cmat_ref[...]
    skip = skip_ref[...]
    chunks = tokens // CHUNK
    span = CHUNK * states
    ones_diag = jnp.where(
        lax.div(lax.broadcasted_iota(jnp.int32, (CHUNK, span), 1), states)
        == lax.broadcasted_iota(jnp.int32, (CHUNK, span), 0),
        1.0,
        0.0,
    ).astype(BF16)

    @pl.when(pl.program_id(0) == 0)
    def _():
        for copy in copies:
            copy.start()
        cols_ref[0] = jnp.zeros(cols_ref.shape[1:], F32)
        cols_ref[1] = out_cols_ref[...]
        spread_to = jnp.where(
            lax.rem(lax.broadcasted_iota(jnp.int32, (states, span), 1), states)
            == lax.broadcasted_iota(jnp.int32, (states, span), 0),
            1.0,
            0.0,
        ).astype(BF16)
        own = lax.div(lax.broadcasted_iota(jnp.int32, (tokens, span), 1), states) == lax.rem(
            lax.broadcasted_iota(jnp.int32, (tokens, span), 0), CHUNK
        )
        by_token = bmat_ref[...].T
        high = by_token.astype(BF16)
        low = (by_token - high.astype(F32)).astype(BF16)
        for part, value in enumerate((high, low)):
            spread = jnp.dot(value, spread_to, preferred_element_type=F32)
            bdiag_s[part] = jnp.where(own, spread, 0.0).astype(BF16)

    def chunk(i, carry):
        running, rate_acc, cols = carry
        base = (chunks - 1 - i) * CHUNK
        for k in reversed(range(CHUNK)):
            t = base + k
            held = slice(k * states, (k + 1) * states)
            stp = step_v[pl.ds(t, 1), block]
            ccol = widen(lane_column(cmat, t), width)
            adjoint = ccol * grad_v[pl.ds(t, 1), block] + running
            adj_s[held, :] = adjoint.astype(BF16)
            partials_s[held, :] = fold_lanes(adjoint * drive_v[pl.ds(t, 1), block])
            running = jnp.exp2(scaled * stp) * adjoint
            prior = before_v[pl.ds(pl.multiple_of(t * states, states), states), block]
            weighted = running * prior.astype(F32)
            rated_s[held, :] = (scaled * weighted).astype(BF16)
            rate_acc = rate_acc + stp * weighted
        rows = pl.ds(pl.multiple_of(base, CHUNK), CHUNK)
        adjoints = adj_s[...]
        driven = jnp.dot(bdiag_s[0, rows, :], adjoints, preferred_element_type=F32)
        driven += jnp.dot(bdiag_s[1, rows, :], adjoints, preferred_element_type=F32)
        rated = jnp.dot(ones_diag, rated_s[...], preferred_element_type=F32)
        input_ref[rows, :] = (step_v[rows, block] * driven + skip * grad_v[rows, block]).astype(BF16)
        stepg_ref[rows, :] = (inp_v[rows, block] * driven + LN2 * rated).astype(BF16)
        return running, rate_acc, lane_sums(base, partials_s, cols)

    beyond = end_ref[...]

    def through(ref, value):
        seed, steps = read_map(ref, states)
        return jnp.exp(-rate * steps) * value + seed

    passed = through(other_ref, beyond)
    beyond = jnp.where(ctx_bit(lax.axis_size("ctx") // 2), passed, beyond)
    enter = through(later_ref, beyond)
    _, rate_acc, cols = lax.fori_loop(
        0, chunks, chunk, (enter, jnp.zeros_like(enter), jnp.zeros(cols_ref.shape[1:], F32))
    )
    rateg_ref[...] = -rate_acc
    cols_ref[0] += cols

    @pl.when(pl.program_id(0) == pl.num_programs(0) - 1)
    def _():
        for copy in copies:
            copy.wait()


def ctx_bit(bit):
    return lax.rem(lax.div(lax.axis_index("ctx"), bit), 2) == 0


def read_map(ref, states):
    held = ref[...].astype(F32)
    steps = held[states : states + 1]
    if ref.dtype == BF16:
        steps = steps + held[states + 1 : states + 2]
    return held[:states], steps


def write_map(seed, steps, out_ref, sent_ref):
    states = seed.shape[0]
    out_ref[:states, :] = seed
    out_ref[states:, :] = steps
    if sent_ref is not None:
        high = steps.astype(BF16).astype(F32)
        sent_ref[...] = jnp.concatenate([seed, high, steps - high], axis=0).astype(BF16)


def fold_kernel(bit, total_ref, later_ref, other_ref, rate_ref, total_out, later_out, sent_out):
    states = rate_ref.shape[0]
    low = ctx_bit(bit)
    rate = rate_ref[...]
    total, other = read_map(total_ref, states), read_map(other_ref, states)

    def after(first, second):
        return jnp.exp(-rate * first[1]) * second[0] + first[0], first[1] + second[1]

    def chosen(one, two):
        return jnp.where(low, one[0], two[0]), jnp.where(low, one[1], two[1])

    write_map(*after(chosen(total, other), chosen(other, total)), total_out, sent_out)
    if later_ref is None:
        later_out[:states, :] = jnp.where(low, other[0], 0.0)
        later_out[states:, :] = jnp.where(low, other[1], 0.0)
    else:
        later = read_map(later_ref, states)
        write_map(*chosen(after(later, other), later), later_out, None)


def first_fold_kernel(bit, total_ref, other_ref, rate_ref, total_out, later_out, sent_out):
    fold_kernel(bit, total_ref, None, other_ref, rate_ref, total_out, later_out, sent_out)


def exchanged_seeds(seeded, decay_rate):
    count = lax.axis_size("ctx")
    states, width = decay_rate.shape
    total, later, totals, sent = seeded, None, [], seeded
    bit = 1
    while bit < count:
        other = lax.ppermute(sent, "ctx", [(i, i ^ bit) for i in range(count)])
        if 2 * bit == count:
            return later, other, totals
        held = [total, other] if later is None else [total, later, other]
        total, later, sent = pl.pallas_call(
            functools.partial(first_fold_kernel if later is None else fold_kernel, bit),
            name=f"fold_{bit}",
            in_specs=[pl.BlockSpec(memory_space=pltpu.VMEM)] * (len(held) + 1),
            out_specs=[pl.BlockSpec(memory_space=pltpu.VMEM)] * 3,
            out_shape=[jax.ShapeDtypeStruct(seeded.shape, F32)] * 2
            + [jax.ShapeDtypeStruct((states + 2, width), BF16)],
            compiler_params=pltpu.CompilerParams(vmem_limit_bytes=SMALL_VMEM),
        )(*held, in_hbm(decay_rate))
        totals.append(total)
        bit *= 2


def scan_call(kernel, name, width, tokens, states, ins, outs, scratch, fetch=None, w_down=None, micros=0):
    block = min(1024, width)
    whole = pl.BlockSpec(memory_space=pltpu.VMEM)
    kinds = {
        "tok": pl.BlockSpec((tokens, block), lambda j: (0, j)),
        "rate": pl.BlockSpec((states, block), lambda j: (0, j)),
        "seed": pl.BlockSpec((states + 1, block), lambda j: (0, j)),
        "sent": pl.BlockSpec((states + 2, block), lambda j: (0, j)),
        "mat": pl.BlockSpec((states, tokens), lambda j: (0, 0)),
        "first": pl.BlockSpec((1, states, block), lambda j: (0, 0, j)),
        "skip": pl.BlockSpec((1, block), lambda j: (0, j)),
        "both": pl.BlockSpec((2, states, tokens), lambda j: (0, 0, 0)),
        "row": whole,
        "state": whole,
    }
    shapes = {
        "tok": jax.ShapeDtypeStruct((tokens, width), BF16),
        "rate": jax.ShapeDtypeStruct((states, width), F32),
        "seed": jax.ShapeDtypeStruct((states + 1, width), F32),
        "mat": jax.ShapeDtypeStruct((states, tokens), F32),
        "both": jax.ShapeDtypeStruct((2, states, tokens), F32),
        "row": pltpu.VMEM((tokens, width), F32),
        "state": pltpu.VMEM((tokens * states, width), BF16),
    }
    scratches = {
        "chunk": pltpu.VMEM((CHUNK * states, block), BF16),
        "sums": pltpu.VMEM((CHUNK * states, LANES), F32),
        "diag": pltpu.VMEM((2, tokens, CHUNK * states), BF16),
    }
    in_specs = [kinds[kind] for kind in ins]
    out_specs = [kinds[kind] for kind in outs]
    out_shape = [shapes[kind] for kind in outs]
    scratch = [scratches[kind] for kind in scratch]
    if fetch is not None:
        hidden = w_down.shape[1]
        in_specs.append(pl.BlockSpec(memory_space=pl.ANY))
        out_specs.append(whole)
        out_shape.append(pltpu.VMEM((fetch[2], hidden, fetch[1]), BF16))
        scratch.append(pltpu.SemaphoreType.DMA((fetch[2],)))
        fetch = (*fetch, len(outs))

    def call(*operands):
        operands = [
            in_vmem(value) if kind in ("row", "state") else value
            for kind, value in zip(ins, operands)
        ]
        if fetch is not None:
            operands.append(in_hbm(w_down))
        return pl.pallas_call(
            kernel if kernel is seed_kernel else functools.partial(kernel, fetch),
            name=name,
            grid=(width // block,),
            in_specs=in_specs,
            out_specs=out_specs,
            out_shape=out_shape,
            scratch_shapes=scratch,
            compiler_params=pltpu.CompilerParams(vmem_limit_bytes=8 * 1024 * 1024),
            cost_estimate=pl.CostEstimate(
                flops=MICRO * micros, bytes_accessed=0, transcendentals=0
            ),
        )(*operands)

    return call


def in_vmem(value):
    return pltpu.with_memory_space_constraint(value, pltpu.VMEM)


def butterfly_sum(value, axis):
    count = lax.axis_size(axis)
    bit = 1
    while bit < count:
        value = value + lax.ppermute(value, axis, [(i, i ^ bit) for i in range(count)])
        bit *= 2
    return value


def pack_kernel(widths, local, capacity, grad_ref, route_ref, gate_ref, *out_refs):
    tokens = route_ref.shape[1]
    around = lax.axis_size("exp")
    place = lax.rem(lax.axis_index("ctx"), 2) * around + lax.axis_index("exp")
    expert = lax.broadcasted_iota(jnp.int32, (EXPERTS, tokens), 0)
    chosen = [expert == route_ref[j : j + 1, :] for j in range(2)]
    named = jnp.where(chosen[0] | chosen[1], 1.0, 0.0).astype(BF16)
    row = lax.broadcasted_iota(jnp.int32, (tokens, tokens), 0)
    col = lax.broadcasted_iota(jnp.int32, (tokens, tokens), 1)
    earlier = jnp.dot(
        named, jnp.where(row < col, 1.0, 0.0).astype(BF16), preferred_element_type=F32
    )
    spot = lax.broadcasted_iota(jnp.int32, (EXTRA, tokens), 0)
    table = jnp.zeros((EXTRA, tokens), F32)
    for j in range(2):
        rank = jnp.sum(jnp.where(chosen[j], earlier, 0.0), axis=0, keepdims=True)
        number = route_ref[j : j + 1, :]
        owner = lax.div(number, local)
        slot = ((number - owner * local) * (2 * around) + place) * capacity
        prob = gate_ref[j : j + 1, :]
        high = prob.astype(BF16).astype(F32)
        middle = (prob - high).astype(BF16).astype(F32)
        low = prob - high - middle
        fields = (owner.astype(F32), slot.astype(F32) + rank, high, middle, low)
        for k, field in enumerate(fields):
            table = jnp.where(spot == 8 * j + k, field, table)
    extra = lax.dot_general(
        jnp.where(row == col, 1.0, 0.0).astype(BF16),
        table.astype(BF16),
        (((1,), (1,)), ((), ())),
        preferred_element_type=F32,
    )
    start = 0
    for width, out_ref in zip(widths, out_refs):
        out_ref[:, :width] = grad_ref[:, start : start + width]
        start += width
    out_refs[0][:, widths[0] :] = extra.astype(BF16)


def in_hbm(value):
    return pltpu.with_memory_space_constraint(value, pltpu.HBM)


def pack_tokens(moe_grad, route, gate_prob, widths, local, capacity):
    tokens = moe_grad.shape[0]
    vmem = pl.BlockSpec(memory_space=pltpu.VMEM)
    outs = [
        jax.ShapeDtypeStruct((tokens, width + (EXTRA if p == 0 else 0)), BF16)
        for p, width in enumerate(widths)
    ]
    return pl.pallas_call(
        functools.partial(pack_kernel, widths, local, capacity),
        name="pack_tokens",
        in_specs=[vmem] * 3,
        out_specs=[vmem] * len(outs),
        out_shape=outs,
        compiler_params=pltpu.CompilerParams(vmem_limit_bytes=SMALL_VMEM),
    )(in_hbm(moe_grad), in_hbm(route.T), in_hbm(gate_prob.T))


def pairing(partner):
    pairs = []
    for i in range(32):
        z, c, y, x = partner(i // 8, (i // 4) % 2, (i // 2) % 2, i % 2)
        pairs.append((i, ((z * 2 + c) * 2 + y) * 2 + x))
    return pairs


Z_HOPS = [pairing(lambda z, c, y, x, j=j: (z ^ j, c, y, x)) for j in (1, 2, 3)]
CORE_HOP = pairing(lambda z, c, y, x: (z, c ^ 1, y, x))
PLANE_ONE = pairing(lambda z, c, y, x: (z, c, y, x ^ 1) if c == 0 else (z, c, y ^ 1, x))
PLANE_TWO = pairing(lambda z, c, y, x: (z, c, y ^ 1, x) if c == 0 else (z, c, y, x ^ 1))


def after(value, *done):
    return lax.optimization_barrier((value, *done))[0]


def z_hops(value):
    return [lax.ppermute(value, BOTH, hop) for hop in Z_HOPS]


def small_call(kernel, name, shape, *operands, dtype=BF16, limit=2 * 1024 * 1024, result=False):
    kept = pl.BlockSpec(memory_space=pltpu.VMEM)
    return pl.pallas_call(
        kernel,
        name=name,
        in_specs=[kept] * len(operands),
        out_specs=kept,
        out_shape=(jax.ShapeDtypeStruct if result else pltpu.VMEM)(shape, dtype),
        compiler_params=pltpu.CompilerParams(vmem_limit_bytes=limit),
        cost_estimate=pl.CostEstimate(flops=0, bytes_accessed=0, transcendentals=0),
    )(*(in_vmem(value) for value in operands))


def add_kernel(one_ref, two_ref, out_ref):
    total = one_ref[...].astype(F32) + two_ref[...].astype(F32)
    out_ref[...] = total.astype(out_ref.dtype)


def added(one, two, dtype=F32, result=False):
    return small_call(add_kernel, "add_two", one.shape, one, two, dtype=dtype, result=result)


def split_add_kernel(one_ref, two_ref, first_ref, second_ref):
    first_ref[...] = one_ref[0] + two_ref[0]
    second_ref[...] = one_ref[1] + two_ref[1]


def split_added(one, two):
    kept = pl.BlockSpec(memory_space=pltpu.VMEM)
    return pl.pallas_call(
        split_add_kernel,
        name="split_add",
        in_specs=[kept] * 2,
        out_specs=[kept] * 2,
        out_shape=[jax.ShapeDtypeStruct(one.shape[1:], one.dtype)] * 2,
        compiler_params=pltpu.CompilerParams(vmem_limit_bytes=2 * 1024 * 1024),
        cost_estimate=pl.CostEstimate(flops=0, bytes_accessed=0, transcendentals=0),
    )(in_vmem(one), in_vmem(two))


def join_z_kernel(*refs):
    for z, ref in enumerate(refs[:-1]):
        refs[-1][z] = ref[...]


def join_z(own, received):
    shape = (1 + len(received), *own.shape)
    return small_call(join_z_kernel, "join_z", shape, own, *received)


def join_plane_kernel(held_ref, received_ref, out_ref):
    zs, tokens, _ = held_ref.shape
    for z in range(zs):
        at = 2 * tokens * z
        out_ref[at : at + tokens, :] = held_ref[z]
        out_ref[at + tokens : at + 2 * tokens, :] = received_ref[z]


def join_plane(held, received):
    zs, tokens, width = held.shape
    return small_call(join_plane_kernel, "join_plane", (2 * zs * tokens, width), held, received)


def build_picks(zs, piece_refs, pick_v, gate_v):
    rows = piece_refs[0].shape[0]
    slots = pick_v.shape[1]
    rows_z = rows // zs
    extra = slice(piece_refs[0].shape[1] - EXTRA, piece_refs[0].shape[1])
    me = lax.axis_index("exp").astype(F32)
    for jz in range(zs):
        held = jnp.concatenate(
            [ref[jz * rows_z : (jz + 1) * rows_z, extra] for ref in piece_refs], axis=0
        )
        table = held.astype(F32).T
        row = lax.broadcasted_iota(jnp.int32, (slots, held.shape[0]), 0).astype(F32)
        pick = jnp.zeros(row.shape, F32)
        gate = jnp.zeros(row.shape, F32)
        for j in range(2):
            owner, slot, high, middle, low = [table[8 * j + k : 8 * j + k + 1, :] for k in range(5)]
            hit = jnp.where(owner == me, slot, -1.0) == row
            pick = jnp.where(hit, 1.0, pick)
            gate = jnp.where(hit, (high + middle) + low, gate)
        pick_v[jz] = pick.astype(BF16)
        gate_v[jz] = jnp.broadcast_to(jnp.sum(gate, axis=1, keepdims=True), (slots, LANES))


def expert_kernel(first, last, at, width, own, *refs):
    piece_refs, refs = refs[:4], refs[4:]
    saved_v, held_v, refs = refs[0], refs[1], refs[2:]
    ready = held_v.shape[0]
    if own:
        w_ref, refs = refs[0], refs[1:]
    if not first:
        pick_v, gate_v, sum_v, refs = refs[0], refs[1], refs[2], refs[4:]
    down_ref, hidden_ref, refs = refs[0], refs[1], refs[2:]
    if first:
        pick_v, gate_v, refs = refs[0], refs[1], refs[2:]
    if own:
        w_v, w_sems, refs = refs[0], refs[1], refs[2:]

        def w_copy(l):
            return pltpu.make_async_copy(
                w_ref.at[ready + l, :, pl.ds(at, width)], w_v.at[l], w_sems.at[l]
            )

        for l in range(w_v.shape[0]):
            w_copy(l).start()
    if last:
        hidden_s, hidden_sems, refs = refs[0], refs[1], refs[2:]
    slots_s, stage_s, out_sems = refs
    local, slots, _ = slots_s.shape
    zs = pick_v.shape[0]
    per_z, rows_z = slots // zs, piece_refs[0].shape[0] // zs
    pieces = width // PIECE

    def out_copy(expert, n):
        return pltpu.make_async_copy(
            stage_s.at[n], down_ref.at[expert, :, pl.ds(at + n * PIECE, PIECE)], out_sems.at[n]
        )

    if first:
        build_picks(zs, piece_refs, pick_v, gate_v)
    own_z = lax.div(lax.axis_index("ctx"), 2)
    for jz in range(zs):
        out_rows = pl.ds(pl.multiple_of((own_z ^ jz) * per_z, per_z), per_z)
        for start in range(0, width, COLUMNS):
            span = slice(start, start + COLUMNS)
            held = jnp.concatenate(
                [ref[jz * rows_z : (jz + 1) * rows_z, span] for ref in piece_refs], axis=0
            )
            chosen = jnp.dot(pick_v[jz], held, preferred_element_type=F32)
            value = (chosen * widen(gate_v[jz], COLUMNS)).astype(BF16)
            for expert in range(local):
                slots_s[expert, out_rows, span] = value[expert * per_z : (expert + 1) * per_z, :]

    def one_expert(fetched, l, _):
        for n in range(pieces):

            @pl.when(l > 0)
            def _():
                out_copy(l - 1, n).wait()

            for start in range(0, PIECE, COLUMNS):
                span = slice(n * PIECE + start, n * PIECE + start + COLUMNS)
                stage_s[n, :, start : start + COLUMNS] = lax.dot_general(
                    saved_v[l],
                    slots_s[l, :, span],
                    (((0,), (0,)), ((), ())),
                    preferred_element_type=F32,
                ).astype(BF16)
            out_copy(l, n).start()
        if fetched:
            w_copy(l - ready).wait()
        part = lax.dot_general(
            slots_s[l],
            w_v[l - ready] if fetched else held_v[l],
            (((1,), (1,)), ((), ())),
            preferred_element_type=F32,
        )
        if not first:
            part = sum_v[l] + part
        if last:
            hidden_s[l] = part.astype(BF16)
            pltpu.make_async_copy(hidden_s.at[l], hidden_ref.at[l], hidden_sems.at[l]).start()
        else:
            hidden_ref[l] = part
        return 0

    lax.fori_loop(0, ready, functools.partial(one_expert, False), 0)
    if own:
        lax.fori_loop(ready, local, functools.partial(one_expert, True), 0)
    for n in range(pieces):
        out_copy(local - 1, n).wait()
    if last:
        for l in range(local):
            pltpu.make_async_copy(hidden_s.at[l], hidden_ref.at[l], hidden_sems.at[l]).wait()


def expert_call(part, parts, at, width, pieces, saved, held_w, w_down, carried):
    local, hidden, full = w_down.shape
    slots = saved.shape[1]
    zs = 4
    rows = pieces[0].shape[0]
    first, last = part == 0, part == parts - 1
    whole = pl.BlockSpec(memory_space=pl.ANY)
    kept = pl.BlockSpec(memory_space=pltpu.VMEM)
    own = local - held_w.shape[0]
    operands = [in_vmem(value) for value in (*pieces, saved, held_w)]
    in_specs = [kept] * 6
    if own:
        operands.append(in_hbm(w_down))
        in_specs.append(whole)
    aliases = {}
    if not first:
        down, total, pick, gate, *_ = carried
        in_specs += [kept] * 3 + [whole]
        operands += [in_vmem(pick), in_vmem(gate), in_vmem(total), down]
        aliases = {len(operands) - 1: 0}
    out_specs, out_shape = [whole], [jax.ShapeDtypeStruct((local, hidden, full), BF16)]
    scratch = []
    if last:
        out_specs.append(whole)
        out_shape.append(jax.ShapeDtypeStruct((local, slots, hidden), BF16))
        scratch += [pltpu.VMEM((local, slots, hidden), BF16), pltpu.SemaphoreType.DMA((local,))]
    else:
        out_specs.append(kept)
        out_shape.append(pltpu.VMEM((local, slots, hidden), F32))
    if first:
        out_specs += [kept] * 2
        out_shape += [
            pltpu.VMEM((zs, local * slots // zs, 4 * rows // zs), BF16),
            pltpu.VMEM((zs, local * slots // zs, LANES), F32),
        ]
    limit = 12 * 1024 * 1024
    if own:
        scratch = [pltpu.VMEM((own, hidden, width), BF16), pltpu.SemaphoreType.DMA((own,)), *scratch]
        limit += 2 * own * hidden * width
    outs = pl.pallas_call(
        functools.partial(expert_kernel, first, last, at, width, own),
        name=f"experts_{part}",
        in_specs=in_specs,
        out_specs=out_specs,
        out_shape=out_shape,
        scratch_shapes=[
            *scratch,
            pltpu.VMEM((local, slots, width), BF16),
            pltpu.VMEM((width // PIECE, hidden, PIECE), BF16),
            pltpu.SemaphoreType.DMA((width // PIECE,)),
        ],
        input_output_aliases=aliases,
        compiler_params=pltpu.CompilerParams(vmem_limit_bytes=limit),
        cost_estimate=pl.CostEstimate(
            flops=EXPERT_COST if first else 0, bytes_accessed=0, transcendentals=0
        ),
    )(*operands)
    return outs


def slot_buffer(moe_grad, route, gate_prob, capacity):
    pair_count = route.shape[0] * route.shape[1]
    weighted = (gate_prob[:, :, None] * moe_grad.astype(F32)[:, None, :]).astype(BF16)
    weighted = weighted.reshape(pair_count, moe_grad.shape[1])
    flat_route = route.reshape(pair_count)
    onehot = (flat_route[:, None] == jnp.arange(EXPERTS, dtype=jnp.int32)[None, :]).astype(jnp.int32)
    ranks = jnp.sum((jnp.cumsum(onehot, axis=0) - onehot) * onehot, axis=1)
    target = flat_route * capacity + ranks
    placing = (target[:, None] == jnp.arange(EXPERTS * capacity, dtype=jnp.int32)[None, :]).astype(BF16)
    buffer = jnp.einsum("ps,pd->sd", placing, weighted, preferred_element_type=F32).astype(BF16)
    return buffer.reshape(EXPERTS, capacity, moe_grad.shape[1])


def experts_by_slots(moe_grad, route, gate_prob, w_down, hidden_saved, capacity):
    buffer = slot_buffer(moe_grad, route, gate_prob, capacity)
    rows = lax.all_to_all(buffer, "exp", split_axis=0, concat_axis=1, tiled=True)
    rows = lax.all_gather(rows, "ctx", axis=1, tiled=True)
    down = jnp.einsum("lrf,lrd->lfd", hidden_saved, rows, preferred_element_type=F32).astype(BF16)
    hidden = jnp.einsum("lrd,lfd->lrf", rows, w_down, preferred_element_type=F32).astype(BF16)
    return down, hidden


def body(
    scan_input, step_size, decay_rate, input_proj, output_proj, skip_gain, block_states, end_grad,
    scan_grad, moe_grad, route, gate_prob, w_down, hidden_saved,
):
    tokens, width = scan_input.shape
    states = decay_rate.shape[0]
    local, _, full = w_down.shape
    capacity = hidden_saved.shape[1] // (lax.axis_size("ctx") * lax.axis_size("exp"))
    by_tokens = lax.axis_size("ctx") == 8 and lax.axis_size("exp") == 4
    call = functools.partial(scan_call, width=width, tokens=tokens, states=states)
    fetches = (None, None)
    if by_tokens:
        widths = WIDTHS
        fetches = ((0, widths[0], local), (widths[0], widths[1], local - 1))
        assert sum(widths) == full
    seeded, steps, drives, inputs, grads = call(
        seed_kernel, "seed_scan", ins=("tok", "tok", "tok", "rate", "mat"),
        outs=("seed", "row", "row", "row", "row"), scratch=(),
    )(*(in_hbm(value) for value in (step_size, scan_input, scan_grad, decay_rate, output_proj)))
    if by_tokens:
        route = after(route, seeded)
        packed = list(pack_tokens(moe_grad, route, gate_prob, widths, local, capacity))
        from_z = [z_hops(packed[0])]
    later, other, totals = exchanged_seeds(seeded, decay_rate)
    if by_tokens:
        block_states = after(block_states, totals[0], packed[0])
    before, out_cols, *held_w = call(
        forward_kernel, "forward_scan",
        ins=("row", "row", "row", "rate", "mat", "first"),
        outs=("state", "mat"), scratch=("sums",), fetch=fetches[0], w_down=w_down,
    )(steps, drives, grads, in_hbm(decay_rate), in_hbm(input_proj), in_hbm(block_states))
    if by_tokens:
        held_0 = join_z(packed[0], [after(value, out_cols, totals[1]) for value in from_z[0]])
        one_0 = lax.ppermute(held_0, BOTH, PLANE_ONE)
        packed[1] = after(packed[1], held_0)
        from_z.append(z_hops(packed[1]))
        held_0 = join_plane(held_0, after(one_0, other))
        two_0 = lax.ppermute(held_0, BOTH, PLANE_TWO)
        core_0 = lax.ppermute(held_0, BOTH, CORE_HOP)
        later = after(later, held_0)
    input_grad, step_grad, both, rate_local, *more_w = call(
        adjoint_kernel, "adjoint_scan",
        ins=(
            "row", "row", "row", "row", "state", "rate", "mat", "mat", "skip", "rate", "seed", "sent",
            "mat",
        ),
        outs=("tok", "tok", "both", "rate"),
        scratch=("chunk", "chunk", "sums", "diag"), fetch=fetches[1], w_down=w_down, micros=ADJOINT,
    )(
        steps, drives, inputs, grads, before, in_hbm(decay_rate), in_hbm(input_proj),
        in_hbm(output_proj), in_hbm(skip_gain[None]), in_hbm(end_grad), later, other, out_cols,
    )
    if by_tokens:
        rate_core = lax.ppermute(rate_local, BOTH, CORE_HOP)
        both_x = lax.ppermute(both, "exp", [(i, i ^ 1) for i in range(4)])
        rate_chip = added(rate_local, rate_core, BF16)
        both_pair = added(both, after(both_x, rate_chip))
        both_y = lax.ppermute(both_pair, "exp", [(i, i ^ 2) for i in range(4)])
        held_1 = join_z(packed[1], [after(value, both_pair) for value in from_z[1]])
        one_1 = lax.ppermute(held_1, BOTH, PLANE_ONE)
        rate_z1 = lax.ppermute(after(rate_chip, held_1), BOTH, Z_HOPS[0])
        rate_pair = added(rate_chip, rate_z1, BF16)
        rate_z2 = lax.ppermute(rate_pair, BOTH, Z_HOPS[1])
        two_0 = after(two_0, rate_pair)
        core_two_0 = lax.ppermute(two_0, BOTH, CORE_HOP)
        held_1 = join_plane(held_1, after(one_1, two_0))
        decay_grad = added(rate_pair, after(rate_z2, held_1), result=True)
        two_1 = lax.ppermute(held_1, BOTH, PLANE_TWO)
        core_1 = lax.ppermute(held_1, BOTH, CORE_HOP)
        carried = expert_call(
            0, 2, 0, widths[0], [held_0, two_0, core_0, after(core_two_0, decay_grad)],
            hidden_saved, held_w[0], w_down, None,
        )
        both = split_added(both_pair, after(both_y, carried[1]))
        two_1 = after(two_1, both[0])
        core_two_1 = lax.ppermute(two_1, BOTH, CORE_HOP)
        down_grad, hidden_grad = expert_call(
            1, 2, widths[0], widths[1], [held_1, two_1, core_1, core_two_1],
            hidden_saved, more_w[0], w_down, carried,
        )
    else:
        both = butterfly_sum(both, "exp")
        decay_grad = butterfly_sum(rate_local, "ctx")
        down_grad, hidden_grad = experts_by_slots(
            moe_grad, route, gate_prob, w_down, hidden_saved, capacity
        )
    return (input_grad, step_grad, both[0], both[1], decay_grad, down_grad, hidden_grad)


def solution(mesh):
    placed = (
        P("ctx", "exp"),
        P("ctx", "exp"),
        P(None, "exp"),
        P(None, "ctx"),
        P(None, "ctx"),
        P("exp"),
        P("ctx", None, "exp"),
        P(None, "exp"),
        P("ctx", "exp"),
        P(("ctx", "exp"), None),
        P(("ctx", "exp"), None),
        P(("ctx", "exp"), None),
        P("exp", "ctx", None),
        P("exp", None, "ctx"),
    )
    return jax.shard_map(
        body,
        mesh=mesh,
        in_specs=placed,
        out_specs=(
            P("ctx", "exp"),
            P("ctx", "exp"),
            P(None, "ctx"),
            P(None, "ctx"),
            P(None, "exp"),
            P("exp", "ctx", None),
            P("exp", None, "ctx"),
        ),
        check_vma=False,
    )
```
